32 devices in a mesh: test: 2 (over core), slab: 16 (over z, y, x).
Axes of the slice: x: 2, y: 2, z: 4, core: 2. Of those that a mesh axis runs over, the one named last changes fastest.
Arguments:
- log_conductivity: float32 [32, 512, 128], P('slab'), may hold values from -4 to 4
- storage: float32 [32, 512, 128], P('slab'), may hold values from 0.1 to 1
- active_mask: int32 [32, 512, 128], P('slab'), may hold values 0 or 1
- heads: float32 [2, 32, 512, 128], P('test', 'slab'), may hold values from -6 to 6
- adjoint_next: float32 [2, 32, 512, 128], P('test', 'slab'), may hold values from -6 to 6
- pump_cells: int32 [2], P('test'), may hold values from 0 to 2097151
- obs_cells: int32 [64], replicated, may hold values from 0 to 2097151
- obs_data: float32 [2, 64], P('test'), may hold values from -6 to 6
Outputs:
- adjoint: float32 [2, 32, 512, 128], P('test', 'slab')
- gradient: float32 [32, 512, 128], P('slab')
The draws below stay inside these ranges and needn't reach their ends.
All inputs are finite; a program needn't handle non-finite values. No bound on the sum of `active_mask` on one device may be relied on, other than what follows from the above.
Results may differ from the reference program's by a relative error of at most 0.0003.
Values sent between devices are 32-bit elements; how exact they have to be, the bound alone decides.
No kernel may reach another device: no remote copies, remote signals or barrier semaphores. Data moves between devices by JAX's collectives and lax.ppermute only.
A program may use at most 64 MiB of HBM per device.

```python
import math
import jax
import jax.numpy as jnp
from jax import lax

NY = 512
NZ = 128
NOBS = 64
ITERS = 3
TESTS = 2
NX = 32


def axis_wave(key_length, key_phase, extent):
    wave_length = jax.random.uniform(key_length, (TESTS, 4), jnp.float32, 16.0, 48.0)
    wave_phase = jax.random.uniform(key_phase, (TESTS, 4), jnp.float32, -math.pi, math.pi)
    position = jnp.arange(extent, dtype=jnp.float32)
    number = 2.0 * math.pi / wave_length
    return jnp.cos(number[:, :, None] * position[None, None, :] + wave_phase[:, :, None])


def draw_adjoint_next(key, part):
    subkeys = jax.random.split(key, 8)
    waves_x = axis_wave(subkeys[0], subkeys[1], NX)
    waves_y = axis_wave(subkeys[2], subkeys[3], NY)
    waves_z = axis_wave(subkeys[4], subkeys[5], NZ)
    amplitude = jax.random.uniform(subkeys[6], (TESTS, 4), jnp.float32, 0.9, 1.3)
    smooth = jnp.zeros((TESTS, NX, NY, NZ), jnp.float32)
    for which in range(4):
        smooth = smooth + amplitude[:, which, None, None, None] * waves_x[:, which, :, None, None] * waves_y[:, which, None, :, None] * waves_z[:, which, None, None, :]
    noise = 0.1 * jnp.clip(jax.random.normal(subkeys[7], (TESTS, NX, NY, NZ), jnp.float32), -3.0, 3.0)
    return smooth + noise


def plant(values, own_key, smallest, high):
    place = [jax.random.randint(jax.random.fold_in(own_key, axis), (), 0, length) for axis, length in enumerate(values.shape)]
    longest = values.shape.index(max(values.shape))
    next_to = place[:longest] + [(place[longest] + 1) % values.shape[longest]] + place[longest + 1:]
    return values.at[tuple(place)].set(smallest).at[tuple(next_to)].set(high)


def block_scale(own_key, shape, cuts, least, top_value):
    loudness, own = 1.0, jax.random.fold_in(own_key, 6)
    for axis_at, parts in cuts:
        draws = jnp.exp(jax.random.uniform(jax.random.fold_in(own, axis_at), (parts,), jnp.float32, least / len(cuts), top_value / len(cuts)))
        loudness = loudness * jnp.repeat(draws, shape[axis_at] // parts).reshape([-1 if axis == axis_at else 1 for axis in range(len(shape))])
    return loudness


def scatter_about(own_key, shape, width, bound, pieces=(), held_as=jnp.bfloat16):
    gain = block_scale(own_key, shape, pieces, -0.22, 0.18) if pieces else 1.0
    array = jax.random.normal(own_key, shape, jnp.float32) * width * gain
    return jnp.minimum(jnp.maximum(array, -bound), bound).astype(held_as)


def setup_inputs(seed: int = 0) -> dict:
    streams_of = jax.random.split(jax.random.key(seed), 9)
    log_conductivity = scatter_about(streams_of[0], (NX, NY, NZ), 1.0, 4.0, ((0, 16),), jnp.float32)
    storage = jnp.clip(jnp.exp(math.log(1.0) - 2.3025851 * jax.random.uniform(streams_of[1], (NX, NY, NZ), jnp.float32) ** block_scale(streams_of[1], (NX, NY, NZ), ((0, 16),), -0.2, 0.2)), 0.1, 1.0)
    active_mask = plant((jax.random.randint(streams_of[2], (NX, NY, NZ), 0, 8) < 7).astype(jnp.int32), jax.random.fold_in(streams_of[2], 1), 0, 1)
    heads = scatter_about(streams_of[3], (TESTS, NX, NY, NZ), 1.0, 6.0, ((0, 2), (1, 16)), jnp.float32)
    adjoint_next = draw_adjoint_next(jax.random.fold_in(streams_of[8], 71), 0)
    pump_cells = jax.random.randint(streams_of[5], (TESTS,), 0, NX * NY * NZ).astype(jnp.int32)
    obs_cells = plant(jax.random.randint(streams_of[6], (NOBS,), 0, NX * NY * NZ), jax.random.fold_in(streams_of[6], 1), 0, (NX * NY * NZ) - 1).astype(jnp.int32)
    obs_data = scatter_about(streams_of[7], (TESTS, NOBS), 1.0, 6.0, ((0, 2),), jnp.float32)
    return {"log_conductivity": log_conductivity, "storage": storage, "active_mask": active_mask, "heads": heads, "adjoint_next": adjoint_next, "pump_cells": pump_cells, "obs_cells": obs_cells, "obs_data": obs_data}


WELL_TERM = 4.0


def part_of(v, axis_num, start, length):
    return lax.slice_in_dim(v, start, start + length, axis=axis_num)


def pad_axis(v, axis_num):
    widths = [(0, 0)] * v.ndim
    widths[axis_num] = (1, 1)
    return jnp.pad(v, widths)


def face_values(cond_pad, axis_num):
    count = cond_pad.shape[axis_num] - 1
    left = part_of(cond_pad, axis_num, 0, count)
    right = part_of(cond_pad, axis_num, 1, count)
    return 2.0 * left * right / (left + right)


def flux_axis(padded, faces, axis_num):
    count = padded.shape[axis_num] - 1
    terms = faces * (part_of(padded, axis_num, 0, count) - part_of(padded, axis_num, 1, count))
    return part_of(terms, axis_num, 1, count - 1) - part_of(terms, axis_num, 0, count - 1)


def face_total(faces, axis_num):
    count = faces.shape[axis_num] - 1
    return part_of(faces, axis_num, 1, count) + part_of(faces, axis_num, 0, count)


def operate(field, field_x, faces, self_term, active):
    flux = flux_axis(field_x, faces[0], 0)
    flux = flux + flux_axis(pad_axis(field, 1), faces[1], 1)
    flux = flux + flux_axis(pad_axis(field, 2), faces[2], 2)
    return active * (self_term * field + flux) + (1.0 - active) * field


def slope(own, other):
    total = own + other
    return 2.0 * own * other * other / (total * total)


def side_terms(cond_pad, adj_pad, head_pad, axis_num):
    count = cond_pad.shape[axis_num] - 2
    cond_c = part_of(cond_pad, axis_num, 1, count)
    adj_c = part_of(adj_pad, axis_num, 1, count)
    head_c = part_of(head_pad, axis_num, 1, count)
    total = jnp.zeros(cond_c.shape, jnp.float32)
    for start in (0, 2):
        cond_n = part_of(cond_pad, axis_num, start, count)
        adj_n = part_of(adj_pad, axis_num, start, count)
        head_n = part_of(head_pad, axis_num, start, count)
        total = total + slope(cond_c, cond_n) * (adj_c - adj_n) * (head_c - head_n)
    return total


def reference(log_conductivity, storage, active_mask, heads, adjoint_next, pump_cells, obs_cells, obs_data):
    conduct = jnp.exp(log_conductivity)
    active = active_mask.astype(jnp.float32)
    faces = tuple(face_values(pad_axis(conduct, a), a) for a in range(3))
    face_sum = face_total(faces[0], 0) + face_total(faces[1], 1) + face_total(faces[2], 2)
    cond_pads = tuple(pad_axis(conduct, a) for a in range(3))

    def one_test(items):
        heads_t, later_t, pump_t, data_t = items
        well = jnp.zeros((NX * NY * NZ,), jnp.float32).at[pump_t].set(WELL_TERM).reshape(NX, NY, NZ)
        self_term = storage + well
        diag = active * (self_term + face_sum) + (1.0 - active)
        values = heads_t.reshape(-1)[obs_cells] - data_t
        misfit = jnp.zeros((NX * NY * NZ,), jnp.float32).at[obs_cells].add(values).reshape(NX, NY, NZ)
        rhs = active * (storage * later_t + misfit)
        solution = jnp.zeros_like(rhs)
        resid = rhs
        precond = resid / diag
        direction = precond
        rz_now = jnp.sum(resid * precond)
        for step in range(ITERS):
            image = operate(direction, pad_axis(direction, 0), faces, self_term, active)
            alpha = rz_now / jnp.sum(direction * image)
            solution = solution + alpha * direction
            resid = resid - alpha * image
            precond = resid / diag
            rz_next = jnp.sum(resid * precond)
            direction = precond + (rz_next / rz_now) * direction
            rz_now = rz_next
        terms = jnp.zeros_like(rhs)
        for a in range(3):
            terms = terms + side_terms(cond_pads[a], pad_axis(solution, a), pad_axis(heads_t, a), a)
        return solution, -terms

    adjoint, grads = lax.map(one_test, (heads, adjoint_next, pump_cells, obs_data))
    gradient = jnp.sum(grads, axis=0)
    return adjoint, gradient
```

```python
import jax
import jax.numpy as jnp
from jax import lax
from jax.sharding import PartitionSpec as P

WELL_TERM = 4.0


def face_value(a, b):
    return 2.0 * a * b / (a + b)


def slope(own, other):
    total = own + other
    return 2.0 * own * other * other / (total * total)


def shift_down(v, axis):
    widths = [(0, 0)] * v.ndim
    widths[axis] = (1, 0)
    return lax.slice_in_dim(jnp.pad(v, widths), 0, v.shape[axis], axis=axis)


def shift_up(v, axis):
    widths = [(0, 0)] * v.ndim
    widths[axis] = (0, 1)
    return lax.slice_in_dim(jnp.pad(v, widths), 1, v.shape[axis] + 1, axis=axis)


def to_neighbours(low, high):
    count = lax.axis_size("slab")
    before = lax.ppermute(high, "slab", [(i, i + 1) for i in range(count - 1)])
    after = lax.ppermute(low, "slab", [(i + 1, i) for i in range(count - 1)])
    return before, after


def combine(moments, least):
    m0, m1, m2, m3, m4, m5 = moments
    most = 2.0 - least
    alpha_low, alpha_high = 1.0 / most, 1.0 / least
    beta_high = (1.0 - least) * (1.0 - least) / (least * most)

    def alpha_of(rz, curve):
        return jnp.clip(jnp.where(curve > 0.0, rz / curve, alpha_low), alpha_low, alpha_high)

    def beta_of(rz_new, rz):
        return jnp.clip(jnp.where(rz > 0.0, rz_new / rz, 0.0), 0.0, beta_high)

    a0 = alpha_of(m0, m1)
    rz1 = m0 - 2.0 * a0 * m1 + a0 * a0 * m2
    b0 = beta_of(rz1, m0)
    u = 1.0 + b0
    curve1 = u * u * m1 - 2.0 * a0 * u * m2 + a0 * a0 * m3
    a1 = alpha_of(rz1, curve1)
    c1 = -a0 - a1 * u
    c2 = a0 * a1
    rz2 = m0 + 2.0 * c1 * m1 + (2.0 * c2 + c1 * c1) * m2 + 2.0 * c1 * c2 * m3 + c2 * c2 * m4
    b1 = beta_of(rz2, rz1)
    q0 = 1.0 + b1 * u
    q1 = c1 - b1 * a0
    q2 = c2
    curve2 = q0 * q0 * m1 + 2.0 * q0 * q1 * m2 + (2.0 * q0 * q2 + q1 * q1) * m3 + 2.0 * q1 * q2 * m4 + q2 * q2 * m5
    a2 = alpha_of(rz2, curve2)
    return a0 + a1 * u + a2 * q0, a2 * q1 - a1 * a0, a2 * q2


def on_device(
    log_conductivity, storage, active_mask, heads, adjoint_next, pump_cells, obs_cells, obs_data
):
    width, rows, depth = log_conductivity.shape
    slabs = lax.axis_size("slab")
    place = lax.axis_index("slab")
    has_before = place > 0
    has_after = place < slabs - 1
    logs = [log_conductivity[i] for i in range(width)]
    log_before, log_after = to_neighbours(logs[0], logs[-1])
    head = [heads[0, i] for i in range(width)]
    head_before, head_after = to_neighbours(head[0], head[-1])

    cond = [jnp.exp(v) for v in logs]
    cond_before = jnp.where(has_before, jnp.exp(log_before), 0.0)
    cond_after = jnp.where(has_after, jnp.exp(log_after), 0.0)
    active = [active_mask[i].astype(jnp.float32) for i in range(width)]

    row_ids = lax.broadcasted_iota(jnp.int32, (rows, depth), 0)
    lane_ids = lax.broadcasted_iota(jnp.int32, (rows, depth), 1)
    cond_pad = [cond_before, *cond, cond_after]
    face_x = [face_value(cond_pad[i], cond_pad[i + 1]) for i in range(width + 1)]
    face_y = [jnp.where(row_ids > 0, face_value(shift_down(c, 0), c), 0.0) for c in cond]
    face_z = [jnp.where(lane_ids > 0, face_value(shift_down(c, 1), c), 0.0) for c in cond]
    face_sum = [
        face_x[i] + face_x[i + 1] + face_y[i] + shift_up(face_y[i], 0) + face_z[i] + shift_up(face_z[i], 1)
        for i in range(width)
    ]

    cells_here = width * rows * depth
    offset = place * cells_here
    pump_local = pump_cells[0] - offset
    cell_ids = row_ids * depth + lane_ids
    self_term = [
        storage[i] + jnp.where(cell_ids + i * rows * depth == pump_local, WELL_TERM, 0.0).astype(jnp.float32)
        for i in range(width)
    ]
    diag = [active[i] * (self_term[i] + face_sum[i]) + (1.0 - active[i]) for i in range(width)]
    ratio = [jnp.where(active[i] > 0.0, self_term[i] / diag[i], 1.0) for i in range(width)]

    obs_local = obs_cells - offset
    inside = (obs_local >= 0) & (obs_local < cells_here)
    safe_index = jnp.where(inside, obs_local, 0)
    picked = heads[0].reshape(-1)[safe_index]
    values = jnp.where(inside, picked - obs_data[0], 0.0)
    misfit = jnp.zeros((cells_here,), jnp.float32).at[safe_index].add(values).reshape(width, rows, depth)
    rhs = [active[i] * (storage[i] * adjoint_next[0, i] + misfit[i]) for i in range(width)]

    def apply(field, before, after):
        pad = [before, *field, after]
        flux_x = [face_x[i] * (pad[i] - pad[i + 1]) for i in range(width + 1)]
        image = []
        for i in range(width):
            v = field[i]
            flux_y = face_y[i] * (shift_down(v, 0) - v)
            flux_z = face_z[i] * (shift_down(v, 1) - v)
            flux = flux_x[i + 1] - flux_x[i] + shift_up(flux_y, 0) - flux_y + shift_up(flux_z, 1) - flux_z
            image.append(active[i] * (self_term[i] * v + flux))
        return image

    def dot(xs, ys):
        return sum(jnp.sum(x * y, axis=0) for x, y in zip(xs, ys))

    field = [rhs[i] / diag[i] for i in range(width)]
    weighted = rhs
    fields, sums = [], []
    for step in range(3):
        before, after = to_neighbours(field[0], field[-1])
        fields.append([before, *field, after])
        sums.append(dot(field, weighted))
        image = apply(field, before, after)
        sums.append(dot(field, image))
        weighted = image
        field = [image[i] / diag[i] for i in range(width)]
    least = jnp.min(jnp.stack(ratio), axis=(0, 1))
    payload = jnp.stack([*sums, least, least])
    gathered = lax.all_to_all(
        jnp.broadcast_to(payload[None], (slabs, *payload.shape)), "slab", 0, 0, tiled=True
    )
    totals = jnp.sum(jnp.sum(gathered, axis=0), axis=1)
    coefs = combine([totals[i] for i in range(6)], jnp.min(gathered[:, 6]))
    adjoint = [sum(c * f[i] for c, f in zip(coefs, fields)) for i in range(width + 2)]

    head_pad = [head_before, *head, head_after]
    terms = []
    for i in range(width):
        c, a, h = cond[i], adjoint[i + 1], head[i]
        total = jnp.zeros_like(c)
        for j in (i, i + 2):
            total = total + slope(c, cond_pad[j]) * (a - adjoint[j]) * (h - head_pad[j])
        for axis in (0, 1):
            for shift in (shift_down, shift_up):
                total = total + slope(c, shift(c, axis)) * (a - shift(a, axis)) * (h - shift(h, axis))
        terms.append(total)
    terms = -jnp.stack(terms)
    if lax.axis_size("test") == 2:
        gradient = terms + lax.ppermute(terms, "test", [(0, 1), (1, 0)])
    else:
        gradient = lax.psum(terms, "test")
    return jnp.stack(adjoint[1:-1])[None], gradient


def solution(mesh):
    return jax.shard_map(
        on_device,
        mesh=mesh,
        in_specs=(
            P("slab", None, None),
            P("slab", None, None),
            P("slab", None, None),
            P("test", "slab", None, None),
            P("test", "slab", None, None),
            P("test"),
            P(),
            P("test", None),
        ),
        out_specs=(P("test", "slab", None, None), P("slab", None, None)),
        check_vma=False,
    )
```

```python
import jax
import jax.numpy as jnp
from jax import lax
from jax.experimental import pallas as pl
from jax.experimental.pallas import tpu as pltpu
from jax.sharding import PartitionSpec as P

WELL_TERM = 4.0


def face_value(a, b):
    return 2.0 * a * b / (a + b)


def shift_down(v, axis):
    widths = [(0, 0)] * v.ndim
    widths[axis] = (1, 0)
    return lax.slice_in_dim(jnp.pad(v, widths), 0, v.shape[axis], axis=axis)


def shift_up(v, axis):
    widths = [(0, 0)] * v.ndim
    widths[axis] = (0, 1)
    return lax.slice_in_dim(jnp.pad(v, widths), 1, v.shape[axis] + 1, axis=axis)


def to_neighbours(low, high):
    count = lax.axis_size("slab")
    before = lax.ppermute(high, "slab", [(i, i + 1) for i in range(count - 1)])
    after = lax.ppermute(low, "slab", [(i + 1, i) for i in range(count - 1)])
    return before, after


def combine(moments, least):
    m0, m1, m2, m3, m4, m5 = moments
    most = 2.0 - least
    alpha_low, alpha_high = 1.0 / most, 1.0 / least
    beta_high = (1.0 - least) * (1.0 - least) / (least * most)

    def alpha_of(rz, curve):
        return jnp.clip(jnp.where(curve > 0.0, rz / curve, alpha_low), alpha_low, alpha_high)

    def beta_of(rz_new, rz):
        return jnp.clip(jnp.where(rz > 0.0, rz_new / rz, 0.0), 0.0, beta_high)

    a0 = alpha_of(m0, m1)
    rz1 = m0 - 2.0 * a0 * m1 + a0 * a0 * m2
    b0 = beta_of(rz1, m0)
    u = 1.0 + b0
    curve1 = u * u * m1 - 2.0 * a0 * u * m2 + a0 * a0 * m3
    a1 = alpha_of(rz1, curve1)
    c1 = -a0 - a1 * u
    c2 = a0 * a1
    rz2 = m0 + 2.0 * c1 * m1 + (2.0 * c2 + c1 * c1) * m2 + 2.0 * c1 * c2 * m3 + c2 * c2 * m4
    b1 = beta_of(rz2, rz1)
    q0 = 1.0 + b1 * u
    q1 = c1 - b1 * a0
    q2 = c2
    curve2 = q0 * q0 * m1 + 2.0 * q0 * q1 * m2 + (2.0 * q0 * q2 + q1 * q1) * m3 + 2.0 * q1 * q2 * m4 + q2 * q2 * m5
    a2 = alpha_of(rz2, curve2)
    return a0 + a1 * u + a2 * q0, a2 * q1 - a1 * a0, a2 * q2


def coefficient_kernel(parts_ref, coef_ref):
    sums = parts_ref[0]
    least = parts_ref[0]
    for i in range(1, parts_ref.shape[0]):
        sums = sums + parts_ref[i]
        least = jnp.minimum(least, parts_ref[i])
    sums = jnp.sum(sums, axis=1, keepdims=True)
    least = jnp.min(least, axis=1, keepdims=True)
    coefs = combine([sums[i : i + 1] for i in range(6)], least[6:7])
    for i, c in enumerate(coefs):
        coef_ref[i : i + 1, :] = jnp.broadcast_to(c, (1, coef_ref.shape[1]))
    coef_ref[3:8, :] = jnp.zeros((5, coef_ref.shape[1]), jnp.float32)


def coefficients(parts):
    return pl.pallas_call(
        coefficient_kernel,
        out_shape=jax.ShapeDtypeStruct(parts.shape[1:], jnp.float32),
        in_specs=[pl.BlockSpec(memory_space=pltpu.VMEM)],
        out_specs=pl.BlockSpec(memory_space=pltpu.VMEM),
        cost_estimate=pl.CostEstimate(flops=parts.size, bytes_accessed=4 * parts.size, transcendentals=0),
    )(parts)


def shared_halo(low, high):
    if lax.axis_size("test") != 2:
        return to_neighbours(low, high)
    half = low.shape[0] // 2
    test = lax.axis_index("test")
    mine = jnp.stack(to_neighbours(*(lax.dynamic_slice_in_dim(v, test * half, half) for v in (low, high))))
    other = lax.ppermute(mine, "test", [(0, 1), (1, 0)])
    both = jnp.where(test == 0, jnp.concatenate([mine, other], axis=1), jnp.concatenate([other, mine], axis=1))
    return both[0], both[1]


def on_device(
    log_conductivity, storage, active_mask, heads, adjoint_next, pump_cells, obs_cells, obs_data
):
    width, rows, depth = log_conductivity.shape
    slabs = lax.axis_size("slab")
    place = lax.axis_index("slab")
    has_before = place > 0
    has_after = place < slabs - 1
    logs = [log_conductivity[i] for i in range(width)]
    log_before, log_after = shared_halo(logs[0], logs[-1])
    head = [heads[0, i] for i in range(width)]
    head_before, head_after = to_neighbours(head[0], head[-1])

    cond = [jnp.exp(v) for v in logs]
    cond_before = jnp.where(has_before, jnp.exp(log_before), 0.0)
    cond_after = jnp.where(has_after, jnp.exp(log_after), 0.0)
    active = [active_mask[i].astype(jnp.float32) for i in range(width)]

    row_ids = lax.broadcasted_iota(jnp.int32, (rows, depth), 0)
    lane_ids = lax.broadcasted_iota(jnp.int32, (rows, depth), 1)
    cond_pad = [cond_before, *cond, cond_after]
    face_x = [face_value(cond_pad[i], cond_pad[i + 1]) for i in range(width + 1)]
    face_y = [jnp.where(row_ids > 0, face_value(shift_down(c, 0), c), 0.0) for c in cond]
    face_z = [jnp.where(lane_ids > 0, face_value(shift_down(c, 1), c), 0.0) for c in cond]
    face_sum = [
        face_x[i] + face_x[i + 1] + face_y[i] + shift_up(face_y[i], 0) + face_z[i] + shift_up(face_z[i], 1)
        for i in range(width)
    ]

    def edge(face, a, b, head_a, head_b):
        return face * (head_a - head_b) / (a + b)

    head_pad = [head_before, *head, head_after]
    edge_x = [edge(face_x[i], cond_pad[i], cond_pad[i + 1], head_pad[i], head_pad[i + 1]) for i in range(width + 1)]
    edge_y = [edge(face_y[i], shift_down(cond[i], 0), cond[i], shift_down(head[i], 0), head[i]) for i in range(width)]
    edge_z = [edge(face_z[i], shift_down(cond[i], 1), cond[i], shift_down(head[i], 1), head[i]) for i in range(width)]

    cells_here = width * rows * depth
    offset = place * cells_here
    pump_local = pump_cells[0] - offset
    cell_ids = row_ids * depth + lane_ids
    self_term = [
        storage[i] + jnp.where(cell_ids + i * rows * depth == pump_local, WELL_TERM, 0.0).astype(jnp.float32)
        for i in range(width)
    ]
    diag = [active[i] * (self_term[i] + face_sum[i]) + (1.0 - active[i]) for i in range(width)]
    ratio = [jnp.where(active[i] > 0.0, self_term[i] / diag[i], 1.0) for i in range(width)]

    obs_local = obs_cells - offset
    inside = (obs_local >= 0) & (obs_local < cells_here)
    safe_index = jnp.where(inside, obs_local, 0)
    picked = heads[0].reshape(-1)[safe_index]
    values = jnp.where(inside, picked - obs_data[0], 0.0)
    misfit = jnp.zeros((cells_here,), jnp.float32).at[safe_index].add(values).reshape(width, rows, depth)
    rhs = [active[i] * (storage[i] * adjoint_next[0, i] + misfit[i]) for i in range(width)]

    def apply(field, before, after):
        pad = [before, *field, after]
        flux_x = [face_x[i] * (pad[i] - pad[i + 1]) for i in range(width + 1)]
        image = []
        for i in range(width):
            v = field[i]
            flux_y = face_y[i] * (shift_down(v, 0) - v)
            flux_z = face_z[i] * (shift_down(v, 1) - v)
            flux = flux_x[i + 1] - flux_x[i] + shift_up(flux_y, 0) - flux_y + shift_up(flux_z, 1) - flux_z
            image.append(active[i] * (self_term[i] * v + flux))
        return image

    def dot(xs, ys):
        return sum(jnp.sum(x * y, axis=0) for x, y in zip(xs, ys))

    field = [rhs[i] / diag[i] for i in range(width)]
    weighted = rhs
    fields, sums = [], []
    for step in range(3):
        before, after = to_neighbours(field[0], field[-1])
        fields.append([before, *field, after])
        sums.append(dot(field, weighted))
        image = apply(field, before, after)
        sums.append(dot(field, image))
        weighted = image
        field = [image[i] / diag[i] for i in range(width)]
    least = jnp.min(jnp.stack(ratio), axis=(0, 1))
    payload = jnp.stack([*sums, least, least])
    gathered = lax.all_to_all(
        jnp.broadcast_to(payload[None], (slabs, *payload.shape)), "slab", 0, 0, tiled=True
    )
    coefs = coefficients(gathered)
    adjoint = [sum(coefs[k : k + 1] * fields[k][i] for k in range(3)) for i in range(width + 2)]

    terms = []
    for i in range(width):
        a = adjoint[i + 1]
        flux_y = edge_y[i] * (shift_down(a, 0) - a)
        flux_z = edge_z[i] * (shift_down(a, 1) - a)
        total = edge_x[i] * (adjoint[i] - a) * cond_pad[i] + edge_x[i + 1] * (a - adjoint[i + 2]) * cond_pad[i + 2]
        total = total + flux_y * shift_down(cond[i], 0) + shift_up(flux_y * cond[i], 0)
        total = total + flux_z * shift_down(cond[i], 1) + shift_up(flux_z * cond[i], 1)
        terms.append(total)
    terms = -jnp.stack(terms)
    if lax.axis_size("test") == 2:
        gradient = terms + lax.ppermute(terms, "test", [(0, 1), (1, 0)])
    else:
        gradient = lax.psum(terms, "test")
    return jnp.stack(adjoint[1:-1])[None], gradient


def solution(mesh):
    return jax.shard_map(
        on_device,
        mesh=mesh,
        in_specs=(
            P("slab", None, None),
            P("slab", None, None),
            P("slab", None, None),
            P("test", "slab", None, None),
            P("test", "slab", None, None),
            P("test"),
            P(),
            P("test", None),
        ),
        out_specs=(P("test", "slab", None, None), P("slab", None, None)),
        check_vma=False,
    )
```

```python
import jax
import jax.numpy as jnp
from jax import lax
from jax.experimental import pallas as pl
from jax.experimental.pallas import tpu as pltpu
from jax.sharding import PartitionSpec as P

WELL_TERM = 4.0
CHUNK = 64
VMEM = pltpu.VMEM
SMEM = pltpu.SMEM


def row_before(ref, start, count):
    if start == 0:
        return pltpu.roll(ref[0:count], 1, 0)
    return ref[start - 1 : start + count - 1]


def row_after(ref, start, count):
    if start + count == ref.shape[0]:
        return pltpu.roll(ref[start : start + count], count - 1, 0)
    return ref[start + 1 : start + count + 1]


def lane_before(v):
    return pltpu.roll(v, 1, 1)


def lane_after(v):
    return pltpu.roll(v, v.shape[1] - 1, 1)


def chunks_of(rows):
    count = min(CHUNK, rows)
    return [(start, count) for start in range(0, rows, count)]


def fold(v):
    return jnp.sum(v.reshape(v.shape[0] // 8, 8, v.shape[1]), axis=0)


def call(kernel, ins, outs, flops, scalars=0, space=VMEM):
    out_shape = [VMEM(o, jnp.float32) if isinstance(o, tuple) else o for o in outs]
    moved = 4 * sum(x.size for x in ins)
    if space is not None:
        ins = [x if i < scalars else pltpu.with_memory_space_constraint(x, space) for i, x in enumerate(ins)]
    return pl.pallas_call(
        kernel,
        out_shape=out_shape,
        in_specs=[pl.BlockSpec(memory_space=SMEM if i < scalars else VMEM) for i in range(len(ins))],
        out_specs=[pl.BlockSpec(memory_space=VMEM)] * len(outs),
        cost_estimate=pl.CostEstimate(flops=flops, bytes_accessed=moved, transcendentals=0),
        compiler_params=pltpu.CompilerParams(vmem_limit_bytes=16 * 1024 * 1024),
    )(*ins)


def plane_at(i, width, flip):
    return i + flip * (width - 1 - 2 * i)


SIDES = ("y0", "y1", "z0", "z1")


def prepare_kernel(width, place_ref, obs_ref, data_ref, log_ref, storage_ref, mask_ref, head_ref, later_ref, *outs):
    names = ["cond", "own", "base", "rhs", "active", "head", *("f" + s for s in SIDES), *("g" + s for s in SIDES)]
    out = {name: outs[k * width : (k + 1) * width] for k, name in enumerate(names)}
    rest = outs[len(names) * width :]
    fx, gx0, gx1 = (rest[k * (width - 1) : (k + 1) * (width - 1)] for k in range(3))
    rows, depth = outs[0].shape
    at = [plane_at(i, width, place_ref[3]) for i in range(width)]
    for i in range(width):
        for r, n in chunks_of(rows):
            part = slice(r, r + n)
            out["cond"][i][part] = jnp.exp(log_ref[at[i], part])
            out["head"][i][part] = head_ref[0, at[i], part]
    lane = lax.broadcasted_iota(jnp.int32, (min(CHUNK, rows), depth), 1)
    row = lax.broadcasted_iota(jnp.int32, (min(CHUNK, rows), depth), 0)
    for i in range(width):
        cond_i, head_i = out["cond"][i], out["head"][i]
        for r, n in chunks_of(rows):
            part = slice(r, r + n)
            c, h = cond_i[part], head_i[part]

            def pair(cond_n, head_n, inside=None):
                inverse = 1.0 / (c + cond_n)
                face = 2.0 * c * cond_n * inverse
                if inside is not None:
                    face = jnp.where(inside, face, 0.0)
                return face, face * inverse * (h - head_n), cond_n

            well = jnp.where(row * depth + lane + (at[i] * rows + r) * depth == place_ref[0], WELL_TERM, 0.0)
            store = storage_ref[at[i], part]
            own = store + well
            active = mask_ref[at[i], part].astype(jnp.float32)
            out["own"][i][part] = own
            out["active"][i][part] = active
            out["rhs"][i][part] = active * (store * later_ref[0, at[i], part])
            around = {
                "y0": pair(row_before(cond_i, r, n), row_before(head_i, r, n), None if r else row > 0),
                "y1": pair(row_after(cond_i, r, n), row_after(head_i, r, n), None if r + n < rows else row < n - 1),
                "z0": pair(lane_before(c), lane_before(h), lane > 0),
                "z1": pair(lane_after(c), lane_after(h), lane < depth - 1),
            }
            base = own
            for side, (face, slope, cond_n) in around.items():
                out["f" + side][i][part] = face
                out["g" + side][i][part] = slope * cond_n
                base = base + face
            if i > 0:
                base = base + fx[i - 1][part]
            if i < width - 1:
                cond_n = out["cond"][i + 1][part]
                face, slope, _ = pair(cond_n, out["head"][i + 1][part])
                fx[i][part] = face
                gx1[i][part] = slope * cond_n
                gx0[i][part] = -slope * c
                base = base + face
            out["base"][i][part] = base
    lanes = lax.broadcasted_iota(jnp.int32, (1, depth), 1)

    def observe(o, _):
        local = obs_ref[o] - place_ref[4]
        for i in range(width):
            cell = local - at[i] * rows * depth

            @pl.when((cell >= 0) & (cell < rows * depth))
            def _():
                line = pl.ds(cell // depth, 1)
                here = (lanes == cell % depth) & (out["active"][i][line] > 0.0)
                out["rhs"][i][line] += jnp.where(here, out["head"][i][line] - data_ref[o], 0.0)

        return 0

    lax.fori_loop(0, obs_ref.shape[0], observe, 0)


def start_kernel(width, place_ref, *refs):
    mine, others = refs[:2], refs[2:4]
    cond, base, own, rhs, active = (refs[4 + k * width : 4 + (k + 1) * width] for k in range(5))
    refs = refs[4 + 5 * width :]
    field, inverse, outer, outer_slope = refs[:width], refs[width : 2 * width], refs[2 * width : 2 * width + 2], refs[2 * width + 2 : 2 * width + 4]
    sums_ref, least_ref = refs[2 * width + 4 :]
    rows, depth = base[0].shape
    half = mine[0].shape[0]
    sums = jnp.zeros((8, depth), jnp.float32)
    least = jnp.ones((8, depth), jnp.float32)
    for r, n in chunks_of(rows):
        part = slice(r, r + n)
        from_half = slice(r % half, r % half + n)
        mine_here = place_ref[5] == r // half
        faces = []
        for k, i in enumerate((0, width - 1)):
            c = cond[i][part]
            log_n = mine[k][from_half]
            if half < rows:
                log_n = jnp.where(mine_here, log_n, others[k][from_half])
            cond_n = jnp.exp(log_n)
            ratio = cond_n / (c + cond_n)
            face = jnp.where(place_ref[1 + k] > 0, 2.0 * c * ratio, 0.0)
            outer[k][part] = face
            outer_slope[k][part] = face * ratio
            faces.append(face)
        for i in range(width):
            total = base[i][part]
            if i == 0:
                total = total + faces[0]
            if i == width - 1:
                total = total + faces[1]
            here = active[i][part] > 0.0
            inv = 1.0 / total
            least_here = jnp.where(here, own[i][part] * inv, 1.0)
            inv = jnp.where(here, inv, 0.0)
            right = rhs[i][part]
            v = right * inv
            field[i][part] = v
            inverse[i][part] = inv
            sums = sums + fold(v * right)
            least = jnp.minimum(least, jnp.min(least_here.reshape(n // 8, 8, depth), axis=0))
    sums_ref[...] = sums
    least_ref[...] = least


def inner_kernel(width, *refs):
    count = 2 + 2 * len(SIDES)
    v, own, *coefs = (refs[k * width : (k + 1) * width] for k in range(count))
    rest = refs[count * width :]
    fx, gx0, gx1 = (rest[k * (width - 1) : (k + 1) * (width - 1)] for k in range(3))
    outs = rest[3 * (width - 1) :]
    image, terms = outs[:width], outs[width:]
    faces, slopes = coefs[: len(SIDES)], coefs[len(SIDES) :]
    rows = v[0].shape[0]
    for i in range(width):
        for r, n in chunks_of(rows):
            part = slice(r, r + n)
            here = v[i][part]
            total = own[i][part] * here
            term = jnp.zeros_like(here)
            around = (row_before(v[i], r, n), row_after(v[i], r, n), lane_before(here), lane_after(here))
            for k, other in enumerate(around):
                step = here - other
                total = total + faces[k][i][part] * step
                term = term + slopes[k][i][part] * step
            if i > 0:
                step = here - v[i - 1][part]
                total = total + fx[i - 1][part] * step
                term = term + gx0[i - 1][part] * step
            if i < width - 1:
                step = here - v[i + 1][part]
                total = total + fx[i][part] * step
                term = term + gx1[i][part] * step
            image[i][part] = total
            terms[i][part] = term


def outer_image(width, refs, part):
    inner, v, outer, halo = refs
    result = []
    for i in range(width):
        w, here = inner[i][part], v[i][part]
        if i == 0:
            w = w + outer[0][part] * (here - halo[0][part])
        if i == width - 1:
            w = w + outer[1][part] * (here - halo[1][part])
        result.append((here, w))
    return result


def edge_kernel(width, *refs):
    slope, head, heads_halo = refs[:2], refs[2 : 2 + width], refs[2 + width : 4 + width]
    refs = refs[4 + width :]
    count = (len(refs) - 2) // (3 * width + 2)
    sets = [refs[k * (2 * width + 2) : (k + 1) * (2 * width + 2)] for k in range(count)]
    weight, outs = refs[count * (2 * width + 2) :][:2], refs[count * (2 * width + 2) + 2 :]
    rows = slope[0].shape[0]
    for r, n in chunks_of(rows):
        part = slice(r, r + n)
        for k, i in enumerate((0, width - 1)):
            weight[k][part] = slope[k][part] * (head[i][part] - heads_halo[k][part])
        for j, (*arrays,) in enumerate(sets):
            v, halo, terms = arrays[:width], arrays[width : width + 2], arrays[width + 2 :]
            for i in range(width):
                outs[j * width + i][part] = outer_term(width, i, terms, v, halo, weight, part)


def outer_term(width, i, terms, v, halo, weight, part):
    term = terms[i][part]
    for k, end in enumerate((0, width - 1)):
        if i == end:
            term = term + weight[k][part] * (v[i][part] - halo[k][part])
    return term


def finish_kernel(width, *refs):
    inner, v, inverse = (refs[k * width : (k + 1) * width] for k in range(3))
    outer, halo = refs[3 * width : 3 * width + 2], refs[3 * width + 2 : 3 * width + 4]
    following = refs[3 * width + 4 : 4 * width + 4]
    odd_ref, even_ref = refs[4 * width + 4 :]
    rows, depth = v[0].shape
    odd = jnp.zeros((8, depth), jnp.float32)
    even = jnp.zeros((8, depth), jnp.float32)
    for r, n in chunks_of(rows):
        part = slice(r, r + n)
        for i, (here, w) in enumerate(outer_image(width, (inner, v, outer, halo), part)):
            new = w * inverse[i][part]
            following[i][part] = new
            odd = odd + fold(here * w)
            even = even + fold(new * w)
    odd_ref[...] = odd
    even_ref[...] = even


def last_kernel(width, *refs):
    inner, v, terms = (refs[k * width : (k + 1) * width] for k in range(3))
    outer, halo, weight = (refs[3 * width + 2 * k : 3 * width + 2 * k + 2] for k in range(3))
    refs = refs[3 * width + 6 :]
    earlier, least_ref, out_ref, whole_terms = refs[:5], refs[5], refs[6], refs[7:]
    rows, depth = v[0].shape
    odd = jnp.zeros((8, depth), jnp.float32)
    for r, n in chunks_of(rows):
        part = slice(r, r + n)
        for i, (here, w) in enumerate(outer_image(width, (inner, v, outer, halo), part)):
            odd = odd + fold(here * w)
            whole_terms[i][part] = outer_term(width, i, terms, v, halo, weight, part)
    sums = [jnp.sum(x, axis=0, keepdims=True) for x in (*(e[...] for e in earlier), odd)]
    least = jnp.min(least_ref[...], axis=0, keepdims=True)
    told = jnp.concatenate([*sums, least, least], axis=0)
    for k in range(out_ref.shape[0]):
        out_ref[k] = told


def combine(moments, least):
    m0, m1, m2, m3, m4, m5 = moments
    most = 2.0 - least
    alpha_low, alpha_high = 1.0 / most, 1.0 / least
    beta_high = (1.0 - least) * (1.0 - least) / (least * most)

    def alpha_of(rz, curve):
        return jnp.clip(jnp.where(curve > 0.0, rz / curve, alpha_low), alpha_low, alpha_high)

    def beta_of(rz_new, rz):
        return jnp.clip(jnp.where(rz > 0.0, rz_new / rz, 0.0), 0.0, beta_high)

    a0 = alpha_of(m0, m1)
    rz1 = m0 - 2.0 * a0 * m1 + a0 * a0 * m2
    b0 = beta_of(rz1, m0)
    u = 1.0 + b0
    curve1 = u * u * m1 - 2.0 * a0 * u * m2 + a0 * a0 * m3
    a1 = alpha_of(rz1, curve1)
    c1 = -a0 - a1 * u
    c2 = a0 * a1
    rz2 = m0 + 2.0 * c1 * m1 + (2.0 * c2 + c1 * c1) * m2 + 2.0 * c1 * c2 * m3 + c2 * c2 * m4
    b1 = beta_of(rz2, rz1)
    q0 = 1.0 + b1 * u
    q1 = c1 - b1 * a0
    q2 = c2
    curve2 = q0 * q0 * m1 + 2.0 * q0 * q1 * m2 + (2.0 * q0 * q2 + q1 * q1) * m3 + 2.0 * q1 * q2 * m4 + q2 * q2 * m5
    a2 = alpha_of(rz2, curve2)
    return a0 + a1 * u + a2 * q0, a2 * q1 - a1 * a0, a2 * q2


def result_kernel(width, place_ref, told_ref, *refs):
    fields = [refs[k * width : (k + 1) * width] for k in range(3)]
    terms = [refs[k * width : (k + 1) * width] for k in range(3, 6)]
    adjoint_ref, gradient_ref = refs[6 * width :]
    sums = told_ref[0]
    least = told_ref[0]
    for k in range(1, told_ref.shape[0]):
        sums = sums + told_ref[k]
        least = jnp.minimum(least, told_ref[k])
    sums = jnp.sum(sums, axis=1, keepdims=True)
    least = jnp.min(least, axis=1, keepdims=True)
    coefs = combine([sums[i : i + 1] for i in range(6)], least[6:7])
    rows, depth = fields[0][0].shape
    wide = [jnp.broadcast_to(c, (8, depth)) for c in coefs]
    for r, n in chunks_of(rows):
        part = slice(r, r + n)
        scale = [jnp.concatenate([c] * (n // 8), axis=0) for c in wide]
        for i in range(width):
            at = plane_at(i, width, place_ref[3])
            adjoint_ref[0, at, part] = sum(c * f[i][part] for c, f in zip(scale, fields))
            gradient_ref[at, part] = -sum(c * t[i][part] for c, t in zip(scale, terms))


def swap_planes(first, last):
    count = lax.axis_size("slab")
    near = [(i, i ^ 1) for i in range(count) if i ^ 1 < count]
    far = [(a, b) for i in range(1, count - 1, 2) for a, b in ((i, i + 1), (i + 1, i))]
    return lax.ppermute(first, "slab", far), lax.ppermute(last, "slab", near)


def on_device(
    log_conductivity, storage, active_mask, heads, adjoint_next, pump_cells, obs_cells, obs_data
):
    width, rows, depth = log_conductivity.shape
    plane = (rows, depth)
    slabs = lax.axis_size("slab")
    place = lax.axis_index("slab")
    test = lax.axis_index("test")
    two_tests = lax.axis_size("test") == 2
    cells_here = width * rows * depth
    offset = place * cells_here
    flip = place % 2
    far_partner = jnp.where(flip == 0, place - 1, place + 1)
    half = rows // 2
    ends = [plane_at(i, width, flip) for i in (0, width - 1)]

    def piece(array, i, start, count):
        return lax.dynamic_slice(array, (ends[i], start, 0), (1, count, depth))[0]

    if two_tests:
        logs = swap_planes(*(piece(log_conductivity, i, test * half, half) for i in range(2)))
    else:
        logs = swap_planes(*(piece(log_conductivity, i, 0, rows) for i in range(2)))
    flags = jnp.stack(
        [
            pump_cells[0] - offset,
            ((far_partner >= 0) & (far_partner < slabs)).astype(jnp.int32),
            (place + 1 - 2 * flip < slabs).astype(jnp.int32),
            flip,
            offset,
            test if two_tests else jnp.int32(0),
        ]
    )
    planes = [plane] * width
    prepared = call(
        lambda *refs: prepare_kernel(width, *refs),
        [flags, obs_cells, obs_data[0], log_conductivity, storage, active_mask, heads, adjoint_next],
        planes * (6 + 2 * len(SIDES)) + [plane] * (3 * (width - 1)),
        100 * cells_here,
        scalars=3,
        space=pltpu.HBM,
    )
    take = lambda k: prepared[k * width : (k + 1) * width]
    cond, own, base, rhs, active, head = (take(k) for k in range(6))
    coefs = prepared[6 * width :]
    if two_tests:
        logs, prepared = lax.optimization_barrier((logs, prepared))
        logs_sent = [lax.ppermute(x, "test", [(0, 1), (1, 0)]) for x in logs]
    else:
        logs_sent = logs
    heads_halo = swap_planes(head[0], head[-1])
    started = call(
        lambda *refs: start_kernel(width, *refs),
        [flags, *logs, *logs_sent, *cond, *base, *own, *rhs, *active],
        planes * 2 + [plane] * 4 + [(8, depth)] * 2,
        20 * cells_here,
        scalars=1,
    )
    field, inverse = started[:width], started[width : 2 * width]
    outer, outer_slope = started[2 * width : 2 * width + 2], started[2 * width + 2 : 2 * width + 4]
    first_sum, least = started[2 * width + 4 :]

    sums, fields, sets = [first_sum], [], []
    for step in range(3):
        halo = swap_planes(field[0], field[-1])
        fields += field
        inner = call(
            lambda *refs: inner_kernel(width, *refs),
            [*field, *own, *coefs],
            planes * 2,
            30 * cells_here,
        )
        image, terms = inner[:width], inner[width:]
        if step == 0:
            halo, heads_halo = lax.optimization_barrier((halo, heads_halo))
        if step < 2:
            sets += [*field, *halo, *terms]
            *field, odd, even = call(
                lambda *refs: finish_kernel(width, *refs),
                [*image, *field, *inverse, *outer, *halo],
                planes + [(8, depth)] * 2,
                10 * cells_here,
            )
            sums += [odd, even]
    stored = jax.ShapeDtypeStruct(plane, jnp.float32)
    weight_0, weight_1, *whole_terms = call(
        lambda *refs: edge_kernel(width, *refs),
        [*outer_slope, *head, *heads_halo, *sets],
        [plane] * 2 + [stored] * (2 * width),
        10 * cells_here,
    )
    told, *last_terms = call(
        lambda *refs: last_kernel(width, *refs),
        [*image, *field, *terms, *outer, *halo, weight_0, weight_1, *sums, least],
        [jax.ShapeDtypeStruct((slabs, 8, depth), jnp.float32)] + [stored] * width,
        5 * cells_here,
    )
    told = lax.all_to_all(told, "slab", 0, 0, tiled=True)
    adjoint, gradient = call(
        lambda *refs: result_kernel(width, *refs),
        [flags, told, *fields, *whole_terms, *last_terms],
        [jax.ShapeDtypeStruct((1, width, rows, depth), jnp.float32), (width, rows, depth)],
        20 * cells_here,
        scalars=1,
        space=None,
    )
    if two_tests:
        gradient = gradient + lax.ppermute(gradient, "test", [(0, 1), (1, 0)])
    else:
        gradient = lax.psum(gradient, "test")
    return adjoint, gradient


def solution(mesh):
    return jax.shard_map(
        on_device,
        mesh=mesh,
        in_specs=(
            P("slab", None, None),
            P("slab", None, None),
            P("slab", None, None),
            P("test", "slab", None, None),
            P("test", "slab", None, None),
            P("test"),
            P(),
            P("test", None),
        ),
        out_specs=(P("test", "slab", None, None), P("slab", None, None)),
        check_vma=False,
    )
```

```python
import jax
import jax.numpy as jnp
from jax import lax
from jax.experimental import pallas as pl
from jax.experimental.pallas import tpu as pltpu
from jax.sharding import PartitionSpec as P

WELL_TERM = 4.0
CHUNK = 64
COST = 1024
HEADS_STEP = 0
VMEM = pltpu.VMEM
SMEM = pltpu.SMEM


def row_before(ref, start, count):
    if start == 0:
        return pltpu.roll(ref[0:count], 1, 0)
    return ref[start - 1 : start + count - 1]


def row_after(ref, start, count):
    if start + count == ref.shape[0]:
        return pltpu.roll(ref[start : start + count], count - 1, 0)
    return ref[start + 1 : start + count + 1]


def lane_before(v):
    return pltpu.roll(v, 1, 1)


def lane_after(v):
    return pltpu.roll(v, v.shape[1] - 1, 1)


def chunks_of(rows):
    count = min(CHUNK, rows)
    return [(start, count) for start in range(0, rows, count)]


def fold(v):
    return jnp.sum(v.reshape(v.shape[0] // 8, 8, v.shape[1]), axis=0)


def call(kernel, ins, outs, scalars=0, space=VMEM, stored=0, scratch=(), cost=COST):
    out_shape = [VMEM(o, jnp.float32) if isinstance(o, tuple) else o for o in outs]
    if space is not None:
        ins = [
            x if x.size == 1 or (i < scalars and space is VMEM) else pltpu.with_memory_space_constraint(x, space) for i, x in enumerate(ins)
        ]
    return pl.pallas_call(
        kernel,
        out_shape=out_shape,
        in_specs=[
            pl.BlockSpec(memory_space=SMEM if i < scalars else VMEM if i < len(ins) - stored else pl.ANY) for i in range(len(ins))
        ],
        out_specs=[pl.BlockSpec(memory_space=VMEM)] * len(outs),
        scratch_shapes=scratch,
        cost_estimate=pl.CostEstimate(flops=COST, bytes_accessed=cost, transcendentals=0),
        compiler_params=pltpu.CompilerParams(vmem_limit_bytes=16 * 1024 * 1024),
    )(*ins)


def plane_at(i, width, flip):
    return i + flip * (width - 1 - 2 * i)


SIDES = 4


def around(ref, part, start, count):
    here = ref[part]
    return row_before(ref, start, count), row_after(ref, start, count), lane_before(here), lane_after(here)


def native_kernel(width, place, pump_ref, obs_ref, data_ref, storage_ref, mask_ref, head_ref, later_ref, far_ref, near_ref):
    rows, depth = storage_ref.shape[1:]
    lane = lax.broadcasted_iota(jnp.int32, (min(CHUNK, rows), depth), 1)
    row = lax.broadcasted_iota(jnp.int32, (min(CHUNK, rows), depth), 0)
    outs = [(far_ref, 0)] + [(near_ref, 2 * i) for i in range(width - 1)]
    places = [plane_at(i, width, place[7]) for i in range(width)]
    for at, (out_ref, k) in zip(places, outs):
        for r, n in chunks_of(rows):
            part = slice(r, r + n)
            active = mask_ref[at, part] > 0
            store = storage_ref[at, part]
            well = jnp.where(row * depth + lane + (at * rows + r) * depth == pump_ref[0] - place[0], WELL_TERM, 0.0)
            out_ref[k, part] = jnp.where(active, store + well, 0.0)
            out_ref[k + 1, part] = jnp.where(active, store * later_ref[0, at, part], 0.0)
    lanes = lax.broadcasted_iota(jnp.int32, (1, depth), 1)

    def observe(o, _):
        cell = obs_ref[o] - place[0]

        @pl.when((cell >= 0) & (cell < width * rows * depth))
        def _():
            for at, (out_ref, k) in zip(places, outs):
                local = cell - at * rows * depth

                @pl.when((local >= 0) & (local < rows * depth))
                def _():
                    line = pl.ds(local // depth, 1)
                    here = (lanes == local % depth) & (mask_ref[at, line] > 0)
                    out_ref[k + 1, line] += jnp.where(here, head_ref[0, at, line] - data_ref[o], 0.0)

        return 0

    lax.fori_loop(0, obs_ref.shape[0], observe, 0)


def pick(place, kept, moved):
    return jnp.where(place[4], moved, kept)


def cond_kernel(width, place, log_ref, log_moved, log_halo, *outs):
    cond, halo = outs[:width], outs[width]
    for r, n in chunks_of(halo.shape[0]):
        halo[r : r + n] = jnp.exp(log_halo[r : r + n])
    for i in range(width):
        at = plane_at(i, width, place[3])
        for r, n in chunks_of(cond[0].shape[0]):
            part = slice(r, r + n)
            cond[i][part] = jnp.exp(pick(place, log_ref[at, part], log_moved[at, part]))


def face_kernel(width, *refs):
    cond, total, refs = refs[:width], refs[width : 2 * width], refs[2 * width :]
    faces, fx = [refs[k * width : (k + 1) * width] for k in range(SIDES)], refs[SIDES * width :]
    rows, depth = cond[0].shape
    lane = lax.broadcasted_iota(jnp.int32, (min(CHUNK, rows), depth), 1)
    row = lax.broadcasted_iota(jnp.int32, (min(CHUNK, rows), depth), 0)
    for i in range(width):
        for r, n in chunks_of(rows):
            part = slice(r, r + n)
            c = cond[i][part]
            inside = (
                None if r else row > 0,
                None if r + n < rows else row < n - 1,
                lane > 0,
                lane < depth - 1,
            )
            amount = fx[i - 1][part] if i > 0 else jnp.zeros_like(c)
            for k, other in enumerate(around(cond[i], part, r, n)):
                face = 2.0 * c * other / (c + other)
                if inside[k] is not None:
                    face = jnp.where(inside[k], face, 0.0)
                faces[k][i][part] = face
                amount = amount + face
            if i < width - 1:
                other = cond[i + 1][part]
                face = 2.0 * c * other / (c + other)
                fx[i][part] = face
                amount = amount + face
            total[i][part] = amount


def start_kernel(count, ends, place, pack_ref, pack_moved, *refs):
    halo, cond, total = refs[: len(ends)], refs[len(ends) :][:count], refs[len(ends) + count :][:count]
    refs = refs[len(ends) + 2 * count :]
    field, inverse, own = (refs[k * count : (k + 1) * count] for k in range(3))
    outer, refs = refs[3 * count :][: len(ends)], refs[3 * count + len(ends) :]
    sums_ref, least_ref = refs[:2]
    rows, depth = cond[0].shape
    sums = jnp.zeros((8, depth), jnp.float32)
    least = jnp.ones((8, depth), jnp.float32)
    for r, n in chunks_of(rows):
        part = slice(r, r + n)
        for i in range(count):
            c, amount = cond[i][part], total[i][part]
            for k, (end, side) in enumerate(ends):
                if i == end:
                    other = halo[k][part]
                    face = jnp.where(place[1 + side], 2.0 * c * other / (c + other), 0.0)
                    outer[k][part] = face
                    amount = amount + face
            own_here = pick(place, pack_ref[2 * i, part], pack_moved[2 * i, part])
            right = pick(place, pack_ref[2 * i + 1, part], pack_moved[2 * i + 1, part])
            active = own_here > 0.0
            inv = 1.0 / (own_here + amount)
            least_here = jnp.where(active, own_here * inv, 1.0)
            inv = jnp.where(active, inv, 0.0)
            v = right * inv
            own[i][part] = own_here
            field[i][part] = v
            inverse[i][part] = inv
            sums = sums + fold(v * right)
            least = jnp.minimum(least, jnp.min(least_here.reshape(n // 8, 8, depth), axis=0))
    sums_ref[...] = sums
    least_ref[...] = least


def inner_kernel(width, *refs):
    v, own, *faces = (refs[k * width : (k + 1) * width] for k in range(2 + SIDES))
    fx, image = refs[(2 + SIDES) * width : -width], refs[-width:]
    for i in range(width):
        for r, n in chunks_of(v[0].shape[0]):
            part = slice(r, r + n)
            here = v[i][part]
            result = own[i][part] * here
            for k, other in enumerate(around(v[i], part, r, n)):
                result = result + faces[k][i][part] * (here - other)
            if i > 0:
                result = result + fx[i - 1][part] * (here - v[i - 1][part])
            if i < width - 1:
                result = result + fx[i][part] * (here - v[i + 1][part])
            image[i][part] = result


def flat(ref):
    return ref.at[0] if len(ref.shape) == 3 else ref


def outer_image(width, refs, part):
    inner, v, outer, halo = refs
    result = []
    for i in range(width):
        w, here = inner[i][part], v[i][part]
        for k, end in enumerate((0, width - 1)):
            if i == end:
                w = w + outer[k][part] * (here - flat(halo[k])[part])
        result.append((here, w))
    return result


def finish_kernel(width, *refs):
    inner, v, inverse = (refs[k * width : (k + 1) * width] for k in range(3))
    outer, halo = refs[3 * width : 3 * width + 2], refs[3 * width + 2 : 3 * width + 4]
    following = refs[3 * width + 4 : 4 * width + 4]
    odd_ref, even_ref = refs[4 * width + 4 :]
    rows, depth = v[0].shape
    odd = jnp.zeros((8, depth), jnp.float32)
    even = jnp.zeros((8, depth), jnp.float32)
    for r, n in chunks_of(rows):
        part = slice(r, r + n)
        for i, (here, w) in enumerate(outer_image(width, (inner, v, outer, halo), part)):
            new = w * inverse[i][part]
            following[i][part] = new
            odd = odd + fold(here * w)
            even = even + fold(new * w)
    odd_ref[...] = odd
    even_ref[...] = even


def head_kernel(width, place, head_ref, head_moved, *head):
    for i in range(width):
        at = plane_at(i, width, place[3])
        for r, n in chunks_of(head[0].shape[0]):
            part = slice(r, r + n)
            head[i][part] = pick(place, head_ref[0, at, part], head_moved[0, at, part])


def gradient_kernel(width, *refs):
    cond, head, *faces = (refs[k * width : (k + 1) * width] for k in range(2 + SIDES))
    refs = refs[(2 + SIDES) * width :]
    fx, refs = refs[: width - 1], refs[width - 1 :]
    outer, heads_halo, refs = refs[:2], refs[2:4], refs[4:]
    v, refs = [refs[k * width : (k + 1) * width] for k in range(3)], refs[3 * width :]
    halos, refs = [refs[:2], refs[2:4]], refs[4:]
    terms, weight = [refs[k * width : (k + 1) * width] for k in range(3)], refs[3 * width :]
    for i in range(width):
        for r, n in chunks_of(cond[0].shape[0]):
            part = slice(r, r + n)
            h = head[i][part]
            here = [f[i][part] for f in v]
            sums = [jnp.zeros_like(h)] * 3
            others = [around(f[i], part, r, n) for f in v]
            for k, head_n in enumerate(around(head[i], part, r, n)):
                face = faces[k][i][part]
                scale = face * face * (h - head_n)
                sums = [s + scale * (a - b[k]) for s, a, b in zip(sums, here, others)]
            for other, face_ref in ((i - 1, fx[i - 1] if i > 0 else None), (i + 1, fx[i] if i < width - 1 else None)):
                if face_ref is not None:
                    face = face_ref[part]
                    scale = face * face * (h - head[other][part])
                    sums = [s + scale * (a - f[other][part]) for s, a, f in zip(sums, here, v)]
            inverse = 0.5 / cond[i][part]
            for k, end in enumerate((0, width - 1)):
                if i == end:
                    face = outer[k][part]
                    scale = face * face * (h - heads_halo[k][part])
                    weight[k][part] = scale * inverse
                    for j in range(2):
                        sums[j] = sums[j] + scale * (here[j] - flat(halos[j][k])[part])
            for t, s in zip(terms, sums):
                t[i][part] = s * inverse


def last_kernel(width, *refs):
    inner, v, terms = (refs[k * width : (k + 1) * width] for k in range(3))
    outer, halo, weight = (refs[3 * width + 2 * k : 3 * width + 2 * k + 2] for k in range(3))
    refs = refs[3 * width + 6 :]
    first, earlier, leasts, out_ref, whole_terms = refs[:2], refs[2:6], refs[6:8], refs[8], refs[9:]
    rows, depth = v[0].shape
    odd = jnp.zeros((8, depth), jnp.float32)
    for r, n in chunks_of(rows):
        part = slice(r, r + n)
        for i, (here, w) in enumerate(outer_image(width, (inner, v, outer, halo), part)):
            odd = odd + fold(here * w)
            term = terms[i][part]
            for k, end in enumerate((0, width - 1)):
                if i == end:
                    term = term + weight[k][part] * (here - flat(halo[k])[part])
            whole_terms[i][part] = term
    every = (first[0][...] + first[1][...], *(e[...] for e in earlier), odd)
    sums = [jnp.sum(x, axis=0, keepdims=True) for x in every]
    least = jnp.min(jnp.minimum(leasts[0][...], leasts[1][...]), axis=0, keepdims=True)
    told = jnp.concatenate([*sums, least, least], axis=0)
    for k in range(out_ref.shape[0]):
        out_ref[k] = told


def combine(moments, least):
    m0, m1, m2, m3, m4, m5 = moments
    most = 2.0 - least
    alpha_low, alpha_high = 1.0 / most, 1.0 / least
    beta_high = (1.0 - least) * (1.0 - least) / (least * most)

    def alpha_of(rz, curve):
        return jnp.clip(jnp.where(curve > 0.0, rz / curve, alpha_low), alpha_low, alpha_high)

    def beta_of(rz_new, rz):
        return jnp.clip(jnp.where(rz > 0.0, rz_new / rz, 0.0), 0.0, beta_high)

    a0 = alpha_of(m0, m1)
    rz1 = m0 - 2.0 * a0 * m1 + a0 * a0 * m2
    b0 = beta_of(rz1, m0)
    u = 1.0 + b0
    curve1 = u * u * m1 - 2.0 * a0 * u * m2 + a0 * a0 * m3
    a1 = alpha_of(rz1, curve1)
    c1 = -a0 - a1 * u
    c2 = a0 * a1
    rz2 = m0 + 2.0 * c1 * m1 + (2.0 * c2 + c1 * c1) * m2 + 2.0 * c1 * c2 * m3 + c2 * c2 * m4
    b1 = beta_of(rz2, rz1)
    q0 = 1.0 + b1 * u
    q1 = c1 - b1 * a0
    q2 = c2
    curve2 = q0 * q0 * m1 + 2.0 * q0 * q1 * m2 + (2.0 * q0 * q2 + q1 * q1) * m3 + 2.0 * q1 * q2 * m4 + q2 * q2 * m5
    a2 = alpha_of(rz2, curve2)
    return a0 + a1 * u + a2 * q0, a2 * q1 - a1 * a0, a2 * q2


def result_kernel(width, groups, place, told_ref, *refs):
    stored, (gradient_ref, adjoint_ref), (fetched, arrived) = refs[: 6 * width], refs[6 * width : -2], refs[-2:]
    fetches = [pltpu.make_async_copy(x, fetched.at[k], arrived.at[k]) for k, x in enumerate(stored)]
    for fetch in fetches:
        fetch.start()
    terms, fields = (
        [[fetched.at[k * width + i] for i in range(width)] for k in range(first, first + 3)] for first in (0, 3)
    )
    found = []
    for g in range(groups):
        sums = least = told_ref[g]
        for k in range(g + groups, told_ref.shape[0], groups):
            sums = sums + told_ref[k]
            least = jnp.minimum(least, told_ref[k])
        sums = jnp.sum(sums, axis=1, keepdims=True)
        least = jnp.min(least, axis=1, keepdims=True)
        found.append(combine([sums[i : i + 1] for i in range(6)], least[6:7]))
    coefs = [jnp.where(place[5] > 0, b, a) for a, b in zip(found[0], found[-1])]
    rows, depth = fetched.shape[1:]
    wide = [jnp.broadcast_to(c, (8, depth)) for c in coefs]
    for fetch in fetches:
        fetch.wait()
    for r, n in chunks_of(rows):
        part = slice(r, r + n)
        scale = [jnp.concatenate([c] * (n // 8), axis=0) for c in wide]
        for i in range(width):
            at = plane_at(i, width, place[3])
            gradient_ref[at, part] = -sum(c * t[i][part] for c, t in zip(scale, terms))
            adjoint_ref[0, at, part] = sum(c * f[i][part] for c, f in zip(scale, fields))


def adjoint_kernel(place, kept, moved, out_ref):
    for i in range(out_ref.shape[1]):
        for r, n in chunks_of(out_ref.shape[2]):
            part = slice(r, r + n)
            out_ref[0, i, part] = pick(place, kept[0, i, part], moved[0, i, part])


def add_kernel(place, own_ref, beside_ref, other_ref, handed_ref, out_ref):
    for i in range(out_ref.shape[0]):
        for r, n in chunks_of(out_ref.shape[1]):
            part = slice(r, r + n)
            here = pick(place, own_ref[i, part], beside_ref[i, part])
            out_ref[i, part] = here + pick(place, handed_ref[i, part], other_ref[i, part])


BOTH = ("test", "slab")


def on_device(
    log_conductivity, storage, active_mask, heads, adjoint_next, pump_cells, obs_cells, obs_data
):
    width, rows, depth = log_conductivity.shape
    plane, stack = (rows, depth), (width, rows, depth)
    slabs = lax.axis_size("slab")
    cells_here = width * rows * depth
    turned = lax.axis_size("test") == 2 and slabs % 2 == 0
    if turned:
        pairs = [(slabs + 2 * j, 2 * j + 1) for j in range(slabs // 2)]
        far_pairs = [(slabs + i, i + 2) for i in range(slabs - 2)]
        near_axis, near = "test", [(0, 1), (1, 0)]
        far_axis, groups = BOTH, 2
        at = lambda t, i: t * slabs + i
        first_far = [
            way
            for j in range(0, slabs - 2, 2)
            for way in (
                (at(0, j + 2), at(1, j)),
                (at(1, j + 2), at(1, j + 1)),
                (at(0, j + 1), at(0, j + 2)),
                (at(1, j + 1), at(0, j + 3)),
            )
        ]
    else:
        pairs = []
        far_pairs = [(i, i + 1) for i in range(1, slabs - 1, 2)]
        near_axis, near = "slab", [(i, i ^ 1) for i in range(slabs) if i ^ 1 < slabs]
        far_axis, groups = "slab", 1
    both_ways = lambda links: [way for a, b in links for way in ((a, b), (b, a))]
    if not turned:
        first_far = both_ways(far_pairs)

    def position():
        place, test = lax.axis_index("slab"), lax.axis_index("test")
        parity = lax.rem(place, 2)
        flip, mine = (test, place - parity + test) if turned else (parity, place)
        far_partner, near_partner = mine - 1 + 2 * flip, mine + 1 - 2 * flip
        return [
            place * cells_here,
            (far_partner >= 0) & (far_partner < slabs),
            near_partner < slabs,
            flip,
            mine != place,
            parity if turned else 0,
            test if turned else 0,
            parity,
        ]

    def move(x):
        return lax.ppermute(x, BOTH, both_ways(pairs)) if turned else x

    def swap_near(x):
        return lax.ppermute(x, near_axis, near)

    def swap_far(x):
        return lax.ppermute(x, far_axis, both_ways(far_pairs))

    def after(x, *others):
        return lax.optimization_barrier((x, others))[0]

    hbm = lambda *shape: pltpu.HBM(shape, jnp.float32)
    planes = [plane] * width

    far_at = plane_at(0, width, position()[7])
    far_plane = lambda x: lax.dynamic_slice(x, (far_at, 0, 0), (1, rows, depth))[0]
    log_moved = move(log_conductivity)
    far_pack, near_pack = call(
        lambda *refs: native_kernel(width, position(), *refs),
        [pump_cells, obs_cells, obs_data[0], storage, active_mask, heads, adjoint_next],
        [(2, rows, depth), (2 * (width - 1), rows, depth)],
        scalars=3,
        space=pltpu.HBM,
    )
    far_moved = move(far_pack)
    log_halo = lax.ppermute(after(far_plane(log_conductivity), far_pack), far_axis, first_far)
    head_far = lax.ppermute(after(far_plane(heads[0]), far_pack), far_axis, first_far)
    *cond, cond_far = call(
        lambda *refs: cond_kernel(width, position(), *refs),
        [log_conductivity, log_moved, log_halo],
        [*planes, plane],
        space=None,
    )
    cond_halo = [cond_far, swap_near(cond[-1])]
    near_moved = move(after(near_pack, *cond))
    near_moved, head_far = lax.optimization_barrier((near_moved, head_far))
    total, faces = (lambda x: (x[:width], x[width:]))(
        call(lambda *refs: face_kernel(width, *refs), cond, planes * (1 + SIDES) + [plane] * (width - 1))
    )
    def start(first, count, ends, pack, pack_moved):
        started = call(
            lambda *refs: start_kernel(count, ends, position(), *refs),
            [pack, pack_moved, *(cond_halo[side] for _, side in ends), *cond[first:][:count], *total[first:][:count]],
            [plane] * (3 * count + len(ends)) + [(8, depth)] * 2,
        )
        return [*(started[k * count : (k + 1) * count] for k in range(3)), started[3 * count :]]

    field, inverse, own, (outer_far, sum_far, least_far) = start(0, 1, [(0, 0)], far_pack, far_moved)
    v_halo = swap_far(field[0])
    field_near, inverse_near, own_near, (outer_near, sum_near, least_near) = start(
        1, width - 1, [(width - 2, 1)], near_pack, near_moved
    )
    field, inverse, own = [*field, *field_near], [*inverse, *inverse_near], [*own, *own_near]
    outer = [outer_far, outer_near]

    sums, fields, halos = [sum_far, sum_near], [], []
    for step in range(3):
        halo = [swap_far(field[0]) if step else v_halo, swap_near(field[-1])]
        fields += field
        image = call(lambda *refs: inner_kernel(width, *refs), [*field, *own, *faces], planes)
        if step == HEADS_STEP:
            heads_moved = move(after(heads, *image))
        if step == 2:
            head = call(lambda *refs: head_kernel(width, position(), *refs), [heads, heads_moved], planes, space=None)
            head_near = swap_near(head[-1])
        if step < 2:
            halos += halo
            made = call(
                lambda *refs: finish_kernel(width, *refs),
                [*image, *field, *inverse, *outer, *halo],
                planes + [(8, depth)] * 2,
            )
            field, (odd, even) = made[:width], made[width:]
            sums += [odd, even]
    *terms, weight_0, weight_1 = call(
        lambda *refs: gradient_kernel(width, *refs),
        [*cond, *head, *faces, *outer, head_far, head_near, *fields, *halos],
        [hbm(*plane)] * (2 * width) + planes + [plane] * 2,
    )
    told, *last_terms = call(
        lambda *refs: last_kernel(width, *refs),
        [*image, *field, *terms[2 * width :], *outer, *halo, weight_0, weight_1, *sums, least_far, least_near],
        [hbm(groups * slabs, 8, depth)] + [hbm(*plane)] * width,
        cost=1 << 24,
    )
    told = lax.all_to_all(told, BOTH if turned else "slab", 0, 0, tiled=True)
    gradient, adjoint = call(
        lambda *refs: result_kernel(width, groups, position(), *refs),
        [told, *(pltpu.with_memory_space_constraint(x, pltpu.HBM) for x in (*terms[: 2 * width], *last_terms)), *fields],
        [stack, (1, *stack) if turned else jax.ShapeDtypeStruct((1, *stack), jnp.float32)],
        space=None,
        stored=6 * width,
        scratch=[VMEM((6 * width, rows, depth), jnp.float32), pltpu.SemaphoreType.DMA((6 * width,))],
    )
    if turned:
        other = move(gradient)
        beside = lax.ppermute(gradient, "test", near)
        handed = lax.ppermute(other, "test", near)
        (gradient,) = call(
            lambda *refs: add_kernel(position(), *refs),
            [gradient, beside, other, handed],
            [jax.ShapeDtypeStruct(stack, jnp.float32)],
        )
        (adjoint,) = call(
            lambda *refs: adjoint_kernel(position(), *refs),
            [adjoint, move(adjoint)],
            [jax.ShapeDtypeStruct((1, *stack), jnp.float32)],
        )
    else:
        gradient = lax.psum(gradient, "test")
    return adjoint, gradient


def solution(mesh):
    return jax.shard_map(
        on_device,
        mesh=mesh,
        in_specs=(
            P("slab", None, None),
            P("slab", None, None),
            P("slab", None, None),
            P("test", "slab", None, None),
            P("test", "slab", None, None),
            P("test"),
            P(),
            P("test", None),
        ),
        out_specs=(P("test", "slab", None, None), P("slab", None, None)),
        check_vma=False,
    )
```

```python
import jax
import jax.numpy as jnp
from jax import lax
from jax.experimental import pallas as pl
from jax.experimental.pallas import tpu as pltpu
from jax.sharding import PartitionSpec as P

WELL_TERM = 4.0
CHUNK = 64
COST = 1024
HEADS_STEP = 0
SPARE = 8
VMEM = pltpu.VMEM
SMEM = pltpu.SMEM


def row_before(ref, start, count):
    if start == 0:
        return pltpu.roll(ref[0:count], 1, 0)
    return ref[start - 1 : start + count - 1]


def row_after(ref, start, count):
    if start + count == ref.shape[0]:
        return pltpu.roll(ref[start : start + count], count - 1, 0)
    return ref[start + 1 : start + count + 1]


def lane_before(v):
    return pltpu.roll(v, 1, 1)


def lane_after(v):
    return pltpu.roll(v, v.shape[1] - 1, 1)


def chunks_of(rows):
    count = min(CHUNK, rows)
    return [(start, count) for start in range(0, rows, count)]


def fold(v):
    return jnp.sum(v.reshape(v.shape[0] // 8, 8, v.shape[1]), axis=0)


def call(kernel, ins, outs, scalars=0, space=VMEM, stored=0, scratch=(), cost=COST):
    out_shape = [VMEM(o, jnp.float32) if isinstance(o, tuple) else o for o in outs]
    if space is not None:
        ins = [
            x if x.size == 1 or (i < scalars and space is VMEM) else pltpu.with_memory_space_constraint(x, space) for i, x in enumerate(ins)
        ]
    return pl.pallas_call(
        kernel,
        out_shape=out_shape,
        in_specs=[
            pl.BlockSpec(memory_space=SMEM if i < scalars else VMEM if i < len(ins) - stored else pl.ANY) for i in range(len(ins))
        ],
        out_specs=[pl.BlockSpec(memory_space=VMEM)] * len(outs),
        scratch_shapes=scratch,
        cost_estimate=pl.CostEstimate(flops=COST, bytes_accessed=cost, transcendentals=0),
        compiler_params=pltpu.CompilerParams(vmem_limit_bytes=16 * 1024 * 1024),
    )(*ins)


def plane_at(i, width, flip):
    return i + flip * (width - 1 - 2 * i)


SIDES = 4


def around(ref, part, start, count):
    here = ref[part]
    return row_before(ref, start, count), row_after(ref, start, count), lane_before(here), lane_after(here)


def native_kernel(width, first, count, place, pump_ref, obs_ref, data_ref, storage_ref, mask_ref, head_ref, later_ref, pack_ref):
    rows, depth = storage_ref.shape[1:]
    lane = lax.broadcasted_iota(jnp.int32, (min(CHUNK, rows), depth), 1)
    row = lax.broadcasted_iota(jnp.int32, (min(CHUNK, rows), depth), 0)
    places = [plane_at(first + i, width, place[7]) for i in range(count)]
    outs = [(pack_ref, 2 * i) for i in range(count)]
    for at, (out_ref, k) in zip(places, outs):
        for r, n in chunks_of(rows):
            part = slice(r, r + n)
            active = mask_ref[at, part] > 0
            store = storage_ref[at, part]
            well = jnp.where(row * depth + lane + (at * rows + r) * depth == pump_ref[0] - place[0], WELL_TERM, 0.0)
            out_ref[k, part] = jnp.where(active, store + well, 0.0)
            out_ref[k + 1, part] = jnp.where(active, store * later_ref[0, at, part], 0.0)
    lanes = lax.broadcasted_iota(jnp.int32, (1, depth), 1)

    def observe(o):
        cell = obs_ref[o] - place[0]

        @pl.when((cell >= 0) & (cell < width * rows * depth))
        def _():
            for at, (out_ref, k) in zip(places, outs):
                local = cell - at * rows * depth

                @pl.when((local >= 0) & (local < rows * depth))
                def _():
                    line = pl.ds(local // depth, 1)
                    here = (lanes == local % depth) & (mask_ref[at, line] > 0)
                    out_ref[k + 1, line] += jnp.where(here, head_ref[0, at, line] - data_ref[o], 0.0)

    for o in range(obs_ref.shape[0]):
        observe(o)


def pick(place, kept, moved):
    return jnp.where(place[4], moved, kept)


def cond_kernel(width, place, log_ref, log_moved, *cond):
    for i in range(width):
        at = plane_at(i, width, place[3])
        for r, n in chunks_of(cond[0].shape[0]):
            part = slice(r, r + n)
            cond[i][part] = jnp.exp(pick(place, log_ref[at, part], log_moved[at, part]))


def face_kernel(width, *refs):
    cond, total, refs = refs[:width], refs[width : 2 * width], refs[2 * width :]
    faces, fx = [refs[k * width : (k + 1) * width] for k in range(SIDES)], refs[SIDES * width :]
    rows, depth = cond[0].shape
    lane = lax.broadcasted_iota(jnp.int32, (min(CHUNK, rows), depth), 1)
    row = lax.broadcasted_iota(jnp.int32, (min(CHUNK, rows), depth), 0)
    for i in range(width):
        for r, n in chunks_of(rows):
            part = slice(r, r + n)
            c = cond[i][part]
            inside = (
                None if r else row > 0,
                None if r + n < rows else row < n - 1,
                lane > 0,
                lane < depth - 1,
            )
            amount = fx[i - 1][part] if i > 0 else jnp.zeros_like(c)
            for k, other in enumerate(around(cond[i], part, r, n)):
                face = 2.0 * c * other / (c + other)
                if inside[k] is not None:
                    face = jnp.where(inside[k], face, 0.0)
                faces[k][i][part] = face
                amount = amount + face
            if i < width - 1:
                other = cond[i + 1][part]
                face = 2.0 * c * other / (c + other)
                fx[i][part] = face
                amount = amount + face
            total[i][part] = amount


def start_kernel(count, ends, place, pack_ref, pack_moved, *refs):
    halo, cond, total = refs[: len(ends)], refs[len(ends) :][:count], refs[len(ends) + count :][:count]
    refs = refs[len(ends) + 2 * count :]
    field, inverse, own = (refs[k * count : (k + 1) * count] for k in range(3))
    outer, refs = refs[3 * count :][: len(ends)], refs[3 * count + len(ends) :]
    sums_ref, least_ref, *sends = refs
    rows, depth = cond[0].shape
    sums = jnp.zeros((8, depth), jnp.float32)
    least = jnp.ones((8, depth), jnp.float32)
    for r, n in chunks_of(rows):
        part = slice(r, r + n)
        for i in range(count):
            c, amount = cond[i][part], total[i][part]
            for k, (end, side) in enumerate(ends):
                if i == end:
                    other = halo[k][part] if side else jnp.exp(halo[k][part])
                    face = jnp.where(place[1 + side], 2.0 * c * other / (c + other), 0.0)
                    outer[k][part] = face
                    amount = amount + face
            own_here = pick(place, pack_ref[2 * i, part], pack_moved[2 * i, part])
            right = pick(place, pack_ref[2 * i + 1, part], pack_moved[2 * i + 1, part])
            active = own_here > 0.0
            inv = 1.0 / (own_here + amount)
            least_here = jnp.where(active, own_here * inv, 1.0)
            inv = jnp.where(active, inv, 0.0)
            v = right * inv
            own[i][part] = own_here
            field[i][part] = v
            inverse[i][part] = inv
            if sends and i == 0:
                sends[0][part] = v
            sums = sums + fold(v * right)
            least = jnp.minimum(least, jnp.min(least_here.reshape(n // 8, 8, depth), axis=0))
    for send in sends:
        send[rows:] = jnp.zeros((send.shape[0] - rows, depth), jnp.float32)
    sums_ref[...] = sums
    least_ref[...] = least


def inner_kernel(width, *refs):
    v, own, *faces = (refs[k * width : (k + 1) * width] for k in range(2 + SIDES))
    fx, image = refs[(2 + SIDES) * width : -width], refs[-width:]
    for i in range(width):
        for r, n in chunks_of(v[0].shape[0]):
            part = slice(r, r + n)
            here = v[i][part]
            result = own[i][part] * here
            for k, other in enumerate(around(v[i], part, r, n)):
                result = result + faces[k][i][part] * (here - other)
            if i > 0:
                result = result + fx[i - 1][part] * (here - v[i - 1][part])
            if i < width - 1:
                result = result + fx[i][part] * (here - v[i + 1][part])
            image[i][part] = result


def flat(ref):
    return ref.at[0] if len(ref.shape) == 3 else ref


def outer_image(width, refs, part):
    inner, v, outer, halo = refs
    result = []
    for i in range(width):
        w, here = inner[i][part], v[i][part]
        for k, end in enumerate((0, width - 1)):
            if i == end:
                w = w + outer[k][part] * (here - flat(halo[k])[part])
        result.append((here, w))
    return result


def finish_kernel(width, *refs):
    inner, v, inverse = (refs[k * width : (k + 1) * width] for k in range(3))
    outer, halo = refs[3 * width : 3 * width + 2], refs[3 * width + 2 : 3 * width + 4]
    following = refs[3 * width + 4 : 4 * width + 4]
    odd_ref, even_ref = refs[4 * width + 4 :]
    rows, depth = v[0].shape
    odd = jnp.zeros((8, depth), jnp.float32)
    even = jnp.zeros((8, depth), jnp.float32)
    for r, n in chunks_of(rows):
        part = slice(r, r + n)
        for i, (here, w) in enumerate(outer_image(width, (inner, v, outer, halo), part)):
            new = w * inverse[i][part]
            following[i][part] = new
            odd = odd + fold(here * w)
            even = even + fold(new * w)
    odd_ref[...] = odd
    even_ref[...] = even


def head_kernel(width, place, head_ref, head_moved, *head):
    for i in range(width):
        at = plane_at(i, width, place[3])
        for r, n in chunks_of(head[0].shape[0]):
            part = slice(r, r + n)
            head[i][part] = pick(place, head_ref[0, at, part], head_moved[0, at, part])


def gradient_kernel(width, *refs):
    cond, head, *faces = (refs[k * width : (k + 1) * width] for k in range(2 + SIDES))
    refs = refs[(2 + SIDES) * width :]
    fx, refs = refs[: width - 1], refs[width - 1 :]
    outer, heads_halo, refs = refs[:2], refs[2:4], refs[4:]
    v, refs = [refs[k * width : (k + 1) * width] for k in range(3)], refs[3 * width :]
    halos, refs = [refs[:2], refs[2:4]], refs[4:]
    terms, weight = [refs[k * width : (k + 1) * width] for k in range(3)], refs[3 * width :]
    for i in range(width):
        for r, n in chunks_of(cond[0].shape[0]):
            part = slice(r, r + n)
            h = head[i][part]
            here = [f[i][part] for f in v]
            sums = [jnp.zeros_like(h)] * 3
            others = [around(f[i], part, r, n) for f in v]
            for k, head_n in enumerate(around(head[i], part, r, n)):
                face = faces[k][i][part]
                scale = face * face * (h - head_n)
                sums = [s + scale * (a - b[k]) for s, a, b in zip(sums, here, others)]
            for other, face_ref in ((i - 1, fx[i - 1] if i > 0 else None), (i + 1, fx[i] if i < width - 1 else None)):
                if face_ref is not None:
                    face = face_ref[part]
                    scale = face * face * (h - head[other][part])
                    sums = [s + scale * (a - f[other][part]) for s, a, f in zip(sums, here, v)]
            inverse = 0.5 / cond[i][part]
            for k, end in enumerate((0, width - 1)):
                if i == end:
                    face = outer[k][part]
                    scale = face * face * (h - heads_halo[k][part])
                    weight[k][part] = scale * inverse
                    for j in range(2):
                        sums[j] = sums[j] + scale * (here[j] - flat(halos[j][k])[part])
            for t, s in zip(terms, sums):
                t[i][part] = s * inverse


def last_kernel(width, *refs):
    inner, v, terms = (refs[k * width : (k + 1) * width] for k in range(3))
    outer, halo, weight = (refs[3 * width + 2 * k : 3 * width + 2 * k + 2] for k in range(3))
    refs = refs[3 * width + 6 :]
    first, earlier, leasts, out_ref, whole_terms = refs[:2], refs[2:6], refs[6:8], refs[8], refs[9:]
    rows, depth = v[0].shape
    odd = jnp.zeros((8, depth), jnp.float32)
    for r, n in chunks_of(rows):
        part = slice(r, r + n)
        for i, (here, w) in enumerate(outer_image(width, (inner, v, outer, halo), part)):
            odd = odd + fold(here * w)
            term = terms[i][part]
            for k, end in enumerate((0, width - 1)):
                if i == end:
                    term = term + weight[k][part] * (here - flat(halo[k])[part])
            whole_terms[i][part] = term
    every = (first[0][...] + first[1][...], *(e[...] for e in earlier), odd)
    sums = [jnp.sum(x, axis=0, keepdims=True) for x in every]
    least = jnp.min(jnp.minimum(leasts[0][...], leasts[1][...]), axis=0, keepdims=True)
    told = jnp.concatenate([*sums, least, least], axis=0)
    for k in range(out_ref.shape[0]):
        out_ref[k] = told


def combine(moments, least):
    m0, m1, m2, m3, m4, m5 = moments
    most = 2.0 - least
    alpha_low, alpha_high = 1.0 / most, 1.0 / least
    beta_high = (1.0 - least) * (1.0 - least) / (least * most)

    def alpha_of(rz, curve):
        return jnp.clip(jnp.where(curve > 0.0, rz / curve, alpha_low), alpha_low, alpha_high)

    def beta_of(rz_new, rz):
        return jnp.clip(jnp.where(rz > 0.0, rz_new / rz, 0.0), 0.0, beta_high)

    a0 = alpha_of(m0, m1)
    rz1 = m0 - 2.0 * a0 * m1 + a0 * a0 * m2
    b0 = beta_of(rz1, m0)
    u = 1.0 + b0
    curve1 = u * u * m1 - 2.0 * a0 * u * m2 + a0 * a0 * m3
    a1 = alpha_of(rz1, curve1)
    c1 = -a0 - a1 * u
    c2 = a0 * a1
    rz2 = m0 + 2.0 * c1 * m1 + (2.0 * c2 + c1 * c1) * m2 + 2.0 * c1 * c2 * m3 + c2 * c2 * m4
    b1 = beta_of(rz2, rz1)
    q0 = 1.0 + b1 * u
    q1 = c1 - b1 * a0
    q2 = c2
    curve2 = q0 * q0 * m1 + 2.0 * q0 * q1 * m2 + (2.0 * q0 * q2 + q1 * q1) * m3 + 2.0 * q1 * q2 * m4 + q2 * q2 * m5
    a2 = alpha_of(rz2, curve2)
    return a0 + a1 * u + a2 * q0, a2 * q1 - a1 * a0, a2 * q2


def weigh(places, coefs, arrays, store):
    for r, n in chunks_of(arrays[0][0].shape[0]):
        part = slice(r, r + n)
        scale = [jnp.concatenate([c] * (n // 8), axis=0) for c in coefs]
        for i, at in enumerate(places):
            store(at, part, sum(c * a[i][part] for c, a in zip(scale, arrays)))


def fetch_all(stored, fetched, arrived, width):
    copies = [pltpu.make_async_copy(x, fetched.at[k], arrived.at[k]) for k, x in enumerate(stored)]
    for copy in copies:
        copy.start()
    return copies, [[fetched.at[k * width + i] for i in range(width)] for k in range(3)]


def gradient_sum_kernel(width, place, told_ref, *refs):
    stored, (gradient_ref, coef_ref, fetched, arrived) = refs[: 3 * width], refs[3 * width :]
    copies, terms = fetch_all(stored, fetched, arrived, width)
    sums = least = told_ref[0]
    for k in range(1, told_ref.shape[0]):
        sums = sums + told_ref[k]
        least = jnp.minimum(least, told_ref[k])
    sums = jnp.sum(sums, axis=1, keepdims=True)
    least = jnp.min(least, axis=1, keepdims=True)
    coefs = combine([sums[i : i + 1] for i in range(6)], least[6:7])
    depth = coef_ref.shape[1]
    for k, c in enumerate(coefs):
        coef_ref[8 * k : 8 * k + 8] = jnp.broadcast_to(c, (8, depth))
    for copy in copies:
        copy.wait()

    def store(at, part, value):
        gradient_ref[at, part] = value

    weigh([plane_at(i, width, place[3]) for i in range(width)], [jnp.broadcast_to(-c, (8, depth)) for c in coefs], terms, store)


def lambda_kernel(width, place, coef_ref, *refs):
    stored, (adjoint_ref, fetched, arrived) = refs[: 3 * width], refs[3 * width :]
    copies, fields = fetch_all(stored, fetched, arrived, width)
    for copy in copies:
        copy.wait()

    def store(at, part, value):
        adjoint_ref[0, at, part] = value

    weigh([plane_at(i, width, place[3]) for i in range(width)], [coef_ref[8 * k : 8 * k + 8] for k in range(3)], fields, store)


def adjoint_kernel(place, kept, moved, out_ref):
    for i in range(out_ref.shape[1]):
        for r, n in chunks_of(out_ref.shape[2]):
            part = slice(r, r + n)
            out_ref[0, i, part] = pick(place, kept[0, i, part], moved[0, i, part])


def add_kernel(place, own_ref, beside_ref, other_ref, handed_ref, out_ref):
    for i in range(out_ref.shape[0]):
        for r, n in chunks_of(out_ref.shape[1]):
            part = slice(r, r + n)
            here = pick(place, own_ref[i, part], beside_ref[i, part])
            out_ref[i, part] = here + pick(place, handed_ref[i, part], other_ref[i, part])


BOTH = ("test", "slab")


def on_device(
    log_conductivity, storage, active_mask, heads, adjoint_next, pump_cells, obs_cells, obs_data
):
    width, rows, depth = log_conductivity.shape
    plane, stack = (rows, depth), (width, rows, depth)
    slabs = lax.axis_size("slab")
    cells_here = width * rows * depth
    turned = lax.axis_size("test") == 2 and slabs % 2 == 0
    if turned:
        pairs = [(slabs + 2 * j, 2 * j + 1) for j in range(slabs // 2)]
        far_pairs = [(slabs + i, i + 2) for i in range(slabs - 2)]
        near_axis, near = "test", [(0, 1), (1, 0)]
        far_axis = BOTH
        same_test = [[t * slabs + i for t in range(2) for i in range(x, slabs, 2)] for x in range(2)]
        at = lambda t, i: t * slabs + i
        first_far = [
            way
            for j in range(0, slabs - 2, 2)
            for way in (
                (at(0, j + 2), at(1, j)),
                (at(1, j + 2), at(1, j + 1)),
                (at(0, j + 1), at(0, j + 2)),
                (at(1, j + 1), at(0, j + 3)),
            )
        ]
    else:
        pairs = []
        far_pairs = [(i, i + 1) for i in range(1, slabs - 1, 2)]
        near_axis, near = "slab", [(i, i ^ 1) for i in range(slabs) if i ^ 1 < slabs]
        far_axis, same_test = "slab", None
    both_ways = lambda links: [way for a, b in links for way in ((a, b), (b, a))]
    if not turned:
        first_far = both_ways(far_pairs)

    def position():
        place, test = lax.axis_index("slab"), lax.axis_index("test")
        parity = lax.rem(place, 2)
        flip, mine = (test, place - parity + test) if turned else (parity, place)
        far_partner, near_partner = mine - 1 + 2 * flip, mine + 1 - 2 * flip
        return [
            place * cells_here,
            (far_partner >= 0) & (far_partner < slabs),
            near_partner < slabs,
            flip,
            mine != place,
            parity if turned else 0,
            test if turned else 0,
            parity,
        ]

    def move(x):
        return lax.ppermute(x, BOTH, both_ways(pairs)) if turned else x

    def swap_near(x):
        return lax.ppermute(x, near_axis, near)

    def swap_far(x):
        return lax.ppermute(x, far_axis, both_ways(far_pairs))

    def after(x, *others):
        return lax.optimization_barrier((x, others))[0]

    hbm = lambda *shape: pltpu.HBM(shape, jnp.float32)
    planes = [plane] * width

    far_at = plane_at(0, width, position()[7])
    far_plane = lambda x: lax.dynamic_slice(x, (far_at, 0, 0), (1, rows, depth))[0]
    log_moved = move(log_conductivity)
    def native(first, count):
        (pack,) = call(
            lambda *refs: native_kernel(width, first, count, position(), *refs),
            [pump_cells, obs_cells, obs_data[0], storage, active_mask, heads, adjoint_next],
            [(2 * count, rows, depth)],
            scalars=3,
            space=pltpu.HBM,
        )
        return pack

    far_pack, near_pack = native(0, 1), native(1, width - 1)
    far_moved = move(far_pack)
    log_halo = lax.ppermute(after(far_plane(log_conductivity), far_pack), far_axis, first_far)
    cond = call(
        lambda *refs: cond_kernel(width, position(), *refs),
        [log_conductivity, log_moved],
        planes,
        space=None,
    )
    cond_halo = [log_halo, swap_near(cond[-1])]
    near_moved = move(after(near_pack, *cond, log_halo))
    total, faces = (lambda x: (x[:width], x[width:]))(
        call(lambda *refs: face_kernel(width, *refs), cond, planes * (1 + SIDES) + [plane] * (width - 1))
    )
    def start(first, count, ends, pack, pack_moved):
        started = call(
            lambda *refs: start_kernel(count, ends, position(), *refs),
            [pack, pack_moved, *(cond_halo[side] for _, side in ends), *cond[first:][:count], *total[first:][:count]],
            [plane] * (3 * count + len(ends)) + [(8, depth)] * 2 + [(rows + SPARE, depth)] * (not first),
        )
        return [*(started[k * count : (k + 1) * count] for k in range(3)), started[3 * count :]]

    field, inverse, own, (outer_far, sum_far, least_far, send) = start(0, 1, [(0, 0)], far_pack, far_moved)
    v_halo = swap_far(send)
    field_near, inverse_near, own_near, (outer_near, sum_near, least_near) = start(
        1, width - 1, [(width - 2, 1)], near_pack, near_moved
    )
    field, inverse, own = [*field, *field_near], [*inverse, *inverse_near], [*own, *own_near]
    outer = [outer_far, outer_near]

    sums, fields, halos = [sum_far, sum_near], [], []
    for step in range(3):
        halo = [swap_far(field[0]) if step else v_halo, swap_near(field[-1])]
        fields += field
        image = call(lambda *refs: inner_kernel(width, *refs), [*field, *own, *faces], planes, cost=(1 << 23) if step == 1 else COST)
        if step == HEADS_STEP:
            heads_moved = move(after(heads, *image))
        if step == 1:
            heads_moved = after(heads_moved, *image)
            head = call(lambda *refs: head_kernel(width, position(), *refs), [heads, heads_moved], planes, space=None)
            head_far, head_near = swap_far(head[0]), swap_near(head[-1])
        if step < 2:
            halos += halo
            made = call(
                lambda *refs: finish_kernel(width, *refs),
                [*image, *field, *inverse, *outer, *halo],
                planes + [(8, depth)] * 2,
            )
            field, (odd, even) = made[:width], made[width:]
            sums += [odd, even]
    *terms, weight_0, weight_1 = call(
        lambda *refs: gradient_kernel(width, *refs),
        [*cond, *head, *faces, *outer, head_far, head_near, *fields, *halos],
        [hbm(*plane)] * (2 * width) + planes + [plane] * 2,
    )
    told, *last_terms = call(
        lambda *refs: last_kernel(width, *refs),
        [*image, *field, *terms[2 * width :], *outer, *halo, weight_0, weight_1, *sums, least_far, least_near],
        [hbm(slabs, 8, depth)] + [hbm(*plane)] * width,
        cost=1 << 24,
    )
    told = lax.all_to_all(told, far_axis, 0, 0, axis_index_groups=same_test, tiled=True)
    fetching = dict(
        space=None,
        stored=3 * width,
        scratch=[VMEM((3 * width, rows, depth), jnp.float32), pltpu.SemaphoreType.DMA((3 * width,))],
    )
    gradient, coefs = call(
        lambda *refs: gradient_sum_kernel(width, position(), *refs),
        [told, *(pltpu.with_memory_space_constraint(x, pltpu.HBM) for x in (*terms[: 2 * width], *last_terms))],
        [stack, (24, depth)],
        **fetching,
    )
    (adjoint,) = call(
        lambda *refs: lambda_kernel(width, position(), *refs),
        [coefs, *fields],
        [(1, *stack) if turned else jax.ShapeDtypeStruct((1, *stack), jnp.float32)],
        **fetching,
    )
    if turned:
        other = move(gradient)
        beside = lax.ppermute(gradient, "test", near)
        handed = lax.ppermute(other, "test", near)
        (gradient,) = call(
            lambda *refs: add_kernel(position(), *refs),
            [gradient, beside, other, handed],
            [jax.ShapeDtypeStruct(stack, jnp.float32)],
        )
        (adjoint,) = call(
            lambda *refs: adjoint_kernel(position(), *refs),
            [adjoint, move(adjoint)],
            [jax.ShapeDtypeStruct((1, *stack), jnp.float32)],
        )
    else:
        gradient = lax.psum(gradient, "test")
    return adjoint, gradient


def solution(mesh):
    return jax.shard_map(
        on_device,
        mesh=mesh,
        in_specs=(
            P("slab", None, None),
            P("slab", None, None),
            P("slab", None, None),
            P("test", "slab", None, None),
            P("test", "slab", None, None),
            P("test"),
            P(),
            P("test", None),
        ),
        out_specs=(P("test", "slab", None, None), P("slab", None, None)),
        check_vma=False,
    )
```

```python
import jax
import jax.numpy as jnp
from jax import lax
from jax.experimental import pallas as pl
from jax.experimental.pallas import tpu as pltpu
from jax.sharding import PartitionSpec as P

WELL_TERM = 4.0
CHUNK = 64
COST = 1024
HEADS_STEP = 0
SPARE = 8
VMEM = pltpu.VMEM
SMEM = pltpu.SMEM


def row_before(ref, start, count):
    if start == 0:
        return pltpu.roll(ref[0:count], 1, 0)
    return ref[start - 1 : start + count - 1]


def row_after(ref, start, count):
    if start + count == ref.shape[0]:
        return pltpu.roll(ref[start : start + count], count - 1, 0)
    return ref[start + 1 : start + count + 1]


def lane_before(v):
    return pltpu.roll(v, 1, 1)


def lane_after(v):
    return pltpu.roll(v, v.shape[1] - 1, 1)


def chunks_of(rows):
    count = min(CHUNK, rows)
    return [(start, count) for start in range(0, rows, count)]


def fold(v):
    return jnp.sum(v.reshape(v.shape[0] // 8, 8, v.shape[1]), axis=0)


def call(kernel, ins, outs, scalars=0, space=VMEM, stored=0, scratch=(), cost=COST):
    out_shape = [VMEM(o, jnp.float32) if isinstance(o, tuple) else o for o in outs]
    if space is not None:
        ins = [
            x if x.size == 1 or (i < scalars and space is VMEM) else pltpu.with_memory_space_constraint(x, space) for i, x in enumerate(ins)
        ]
    return pl.pallas_call(
        kernel,
        out_shape=out_shape,
        in_specs=[
            pl.BlockSpec(memory_space=SMEM if i < scalars else VMEM if i < len(ins) - stored else pl.ANY) for i in range(len(ins))
        ],
        out_specs=[pl.BlockSpec(memory_space=VMEM)] * len(outs),
        scratch_shapes=scratch,
        cost_estimate=pl.CostEstimate(flops=COST, bytes_accessed=cost, transcendentals=0),
        compiler_params=pltpu.CompilerParams(vmem_limit_bytes=16 * 1024 * 1024),
    )(*ins)


def plane_at(i, width, flip):
    return i + flip * (width - 1 - 2 * i)


SIDES = 4


def around(ref, part, start, count):
    here = ref[part]
    return row_before(ref, start, count), row_after(ref, start, count), lane_before(here), lane_after(here)


def native_kernel(width, first, count, place, pump_ref, obs_ref, data_ref, storage_ref, mask_ref, head_ref, later_ref, pack_ref, *copies):
    rows, depth = storage_ref.shape[1:]
    lane = lax.broadcasted_iota(jnp.int32, (min(CHUNK, rows), depth), 1)
    row = lax.broadcasted_iota(jnp.int32, (min(CHUNK, rows), depth), 0)
    places = [plane_at(first + i, width, place[7]) for i in range(count)]
    outs = [(pack_ref, 2 * i) for i in range(count)]
    for at, (out_ref, k) in zip(places, outs):
        for r, n in chunks_of(rows):
            part = slice(r, r + n)
            active = mask_ref[at, part] > 0
            store = storage_ref[at, part]
            well = jnp.where(row * depth + lane + (at * rows + r) * depth == pump_ref[0] - place[0], WELL_TERM, 0.0)
            out_ref[k, part] = jnp.where(active, store + well, 0.0)
            out_ref[k + 1, part] = jnp.where(active, store * later_ref[0, at, part], 0.0)
    for copy in copies:
        for i in range(copy.shape[1]):
            for r, n in chunks_of(rows):
                copy[0, i, r : r + n] = head_ref[0, i, r : r + n]
    lanes = lax.broadcasted_iota(jnp.int32, (1, depth), 1)

    def observe(o):
        cell = obs_ref[o] - place[0]

        @pl.when((cell >= 0) & (cell < width * rows * depth))
        def _():
            for at, (out_ref, k) in zip(places, outs):
                local = cell - at * rows * depth

                @pl.when((local >= 0) & (local < rows * depth))
                def _():
                    line = pl.ds(local // depth, 1)
                    here = (lanes == local % depth) & (mask_ref[at, line] > 0)
                    out_ref[k + 1, line] += jnp.where(here, head_ref[0, at, line] - data_ref[o], 0.0)

    for o in range(obs_ref.shape[0]):
        observe(o)


def pick(place, kept, moved):
    return jnp.where(place[4], moved, kept)


def cond_kernel(width, place, log_ref, log_moved, *cond):
    for i in range(width):
        at = plane_at(i, width, place[3])
        for r, n in chunks_of(cond[0].shape[0]):
            part = slice(r, r + n)
            cond[i][part] = jnp.exp(pick(place, log_ref[at, part], log_moved[at, part]))


def face_kernel(width, *refs):
    cond, total, refs = refs[:width], refs[width : 2 * width], refs[2 * width :]
    faces, fx = [refs[k * width : (k + 1) * width] for k in range(SIDES)], refs[SIDES * width :]
    rows, depth = cond[0].shape
    lane = lax.broadcasted_iota(jnp.int32, (min(CHUNK, rows), depth), 1)
    row = lax.broadcasted_iota(jnp.int32, (min(CHUNK, rows), depth), 0)
    for i in range(width):
        for r, n in chunks_of(rows):
            part = slice(r, r + n)
            c = cond[i][part]
            inside = (
                None if r else row > 0,
                None if r + n < rows else row < n - 1,
                lane > 0,
                lane < depth - 1,
            )
            amount = fx[i - 1][part] if i > 0 else jnp.zeros_like(c)
            for k, other in enumerate(around(cond[i], part, r, n)):
                face = 2.0 * c * other / (c + other)
                if inside[k] is not None:
                    face = jnp.where(inside[k], face, 0.0)
                faces[k][i][part] = face
                amount = amount + face
            if i < width - 1:
                other = cond[i + 1][part]
                face = 2.0 * c * other / (c + other)
                fx[i][part] = face
                amount = amount + face
            total[i][part] = amount


def start_kernel(count, ends, place, pack_ref, pack_moved, *refs):
    halo, cond, total = refs[: len(ends)], refs[len(ends) :][:count], refs[len(ends) + count :][:count]
    refs = refs[len(ends) + 2 * count :]
    field, inverse, own = (refs[k * count : (k + 1) * count] for k in range(3))
    outer, refs = refs[3 * count :][: len(ends)], refs[3 * count + len(ends) :]
    sums_ref, least_ref, *sends = refs
    rows, depth = cond[0].shape
    sums = jnp.zeros((8, depth), jnp.float32)
    least = jnp.ones((8, depth), jnp.float32)
    for r, n in chunks_of(rows):
        part = slice(r, r + n)
        for i in range(count):
            c, amount = cond[i][part], total[i][part]
            for k, (end, side) in enumerate(ends):
                if i == end:
                    other = halo[k][part] if side else jnp.exp(halo[k][part])
                    face = jnp.where(place[1 + side], 2.0 * c * other / (c + other), 0.0)
                    outer[k][part] = face
                    amount = amount + face
            own_here = pick(place, pack_ref[2 * i, part], pack_moved[2 * i, part])
            right = pick(place, pack_ref[2 * i + 1, part], pack_moved[2 * i + 1, part])
            active = own_here > 0.0
            inv = 1.0 / (own_here + amount)
            least_here = jnp.where(active, own_here * inv, 1.0)
            inv = jnp.where(active, inv, 0.0)
            v = right * inv
            own[i][part] = own_here
            field[i][part] = v
            inverse[i][part] = inv
            if sends and i == 0:
                sends[0][part] = v
            sums = sums + fold(v * right)
            least = jnp.minimum(least, jnp.min(least_here.reshape(n // 8, 8, depth), axis=0))
    for send in sends:
        send[rows:] = jnp.zeros((send.shape[0] - rows, depth), jnp.float32)
    sums_ref[...] = sums
    least_ref[...] = least


def inner_kernel(width, *refs):
    v, own, *faces = (refs[k * width : (k + 1) * width] for k in range(2 + SIDES))
    fx, image = refs[(2 + SIDES) * width : -width], refs[-width:]
    for i in range(width):
        for r, n in chunks_of(v[0].shape[0]):
            part = slice(r, r + n)
            here = v[i][part]
            result = own[i][part] * here
            for k, other in enumerate(around(v[i], part, r, n)):
                result = result + faces[k][i][part] * (here - other)
            if i > 0:
                result = result + fx[i - 1][part] * (here - v[i - 1][part])
            if i < width - 1:
                result = result + fx[i][part] * (here - v[i + 1][part])
            image[i][part] = result


def flat(ref):
    return ref.at[0] if len(ref.shape) == 3 else ref


def outer_image(width, refs, part):
    inner, v, outer, halo = refs
    result = []
    for i in range(width):
        w, here = inner[i][part], v[i][part]
        for k, end in enumerate((0, width - 1)):
            if i == end:
                w = w + outer[k][part] * (here - flat(halo[k])[part])
        result.append((here, w))
    return result


def finish_kernel(width, *refs):
    inner, v, inverse = (refs[k * width : (k + 1) * width] for k in range(3))
    outer, halo = refs[3 * width : 3 * width + 2], refs[3 * width + 2 : 3 * width + 4]
    following = refs[3 * width + 4 : 4 * width + 4]
    odd_ref, even_ref = refs[4 * width + 4 :]
    rows, depth = v[0].shape
    odd = jnp.zeros((8, depth), jnp.float32)
    even = jnp.zeros((8, depth), jnp.float32)
    for r, n in chunks_of(rows):
        part = slice(r, r + n)
        for i, (here, w) in enumerate(outer_image(width, (inner, v, outer, halo), part)):
            new = w * inverse[i][part]
            following[i][part] = new
            odd = odd + fold(here * w)
            even = even + fold(new * w)
    odd_ref[...] = odd
    even_ref[...] = even


def head_kernel(width, place, head_ref, head_moved, *head):
    for i in range(width):
        at = plane_at(i, width, place[3])
        for r, n in chunks_of(head[0].shape[0]):
            part = slice(r, r + n)
            head[i][part] = pick(place, head_ref[0, at, part], head_moved[0, at, part])


def gradient_kernel(width, *refs):
    cond, head, *faces = (refs[k * width : (k + 1) * width] for k in range(2 + SIDES))
    refs = refs[(2 + SIDES) * width :]
    fx, refs = refs[: width - 1], refs[width - 1 :]
    outer, heads_halo, refs = refs[:2], refs[2:4], refs[4:]
    v, refs = [refs[k * width : (k + 1) * width] for k in range(3)], refs[3 * width :]
    halos, refs = [refs[:2], refs[2:4]], refs[4:]
    terms, weight = [refs[k * width : (k + 1) * width] for k in range(3)], refs[3 * width :]
    for i in range(width):
        for r, n in chunks_of(cond[0].shape[0]):
            part = slice(r, r + n)
            h = head[i][part]
            here = [f[i][part] for f in v]
            sums = [jnp.zeros_like(h)] * 3
            others = [around(f[i], part, r, n) for f in v]
            for k, head_n in enumerate(around(head[i], part, r, n)):
                face = faces[k][i][part]
                scale = face * face * (h - head_n)
                sums = [s + scale * (a - b[k]) for s, a, b in zip(sums, here, others)]
            for other, face_ref in ((i - 1, fx[i - 1] if i > 0 else None), (i + 1, fx[i] if i < width - 1 else None)):
                if face_ref is not None:
                    face = face_ref[part]
                    scale = face * face * (h - head[other][part])
                    sums = [s + scale * (a - f[other][part]) for s, a, f in zip(sums, here, v)]
            inverse = 0.5 / cond[i][part]
            for k, end in enumerate((0, width - 1)):
                if i == end:
                    face = outer[k][part]
                    scale = face * face * (h - heads_halo[k][part])
                    weight[k][part] = scale * inverse
                    for j in range(2):
                        sums[j] = sums[j] + scale * (here[j] - flat(halos[j][k])[part])
            for t, s in zip(terms, sums):
                t[i][part] = s * inverse


def last_kernel(width, *refs):
    inner, v, terms = (refs[k * width : (k + 1) * width] for k in range(3))
    outer, halo, weight = (refs[3 * width + 2 * k : 3 * width + 2 * k + 2] for k in range(3))
    refs = refs[3 * width + 6 :]
    first, earlier, leasts, out_ref, whole_terms = refs[:2], refs[2:6], refs[6:8], refs[8], refs[9:]
    rows, depth = v[0].shape
    odd = jnp.zeros((8, depth), jnp.float32)
    for r, n in chunks_of(rows):
        part = slice(r, r + n)
        for i, (here, w) in enumerate(outer_image(width, (inner, v, outer, halo), part)):
            odd = odd + fold(here * w)
            term = terms[i][part]
            for k, end in enumerate((0, width - 1)):
                if i == end:
                    term = term + weight[k][part] * (here - flat(halo[k])[part])
            whole_terms[i][part] = term
    every = (first[0][...] + first[1][...], *(e[...] for e in earlier), odd)
    sums = [jnp.sum(x, axis=0, keepdims=True) for x in every]
    least = jnp.min(jnp.minimum(leasts[0][...], leasts[1][...]), axis=0, keepdims=True)
    told = jnp.concatenate([*sums, least, least], axis=0)
    for k in range(out_ref.shape[0]):
        out_ref[k] = told


def combine(moments, least):
    m0, m1, m2, m3, m4, m5 = moments
    most = 2.0 - least
    alpha_low, alpha_high = 1.0 / most, 1.0 / least
    beta_high = (1.0 - least) * (1.0 - least) / (least * most)

    def alpha_of(rz, curve):
        return jnp.clip(jnp.where(curve > 0.0, rz / curve, alpha_low), alpha_low, alpha_high)

    def beta_of(rz_new, rz):
        return jnp.clip(jnp.where(rz > 0.0, rz_new / rz, 0.0), 0.0, beta_high)

    a0 = alpha_of(m0, m1)
    rz1 = m0 - 2.0 * a0 * m1 + a0 * a0 * m2
    b0 = beta_of(rz1, m0)
    u = 1.0 + b0
    curve1 = u * u * m1 - 2.0 * a0 * u * m2 + a0 * a0 * m3
    a1 = alpha_of(rz1, curve1)
    c1 = -a0 - a1 * u
    c2 = a0 * a1
    rz2 = m0 + 2.0 * c1 * m1 + (2.0 * c2 + c1 * c1) * m2 + 2.0 * c1 * c2 * m3 + c2 * c2 * m4
    b1 = beta_of(rz2, rz1)
    q0 = 1.0 + b1 * u
    q1 = c1 - b1 * a0
    q2 = c2
    curve2 = q0 * q0 * m1 + 2.0 * q0 * q1 * m2 + (2.0 * q0 * q2 + q1 * q1) * m3 + 2.0 * q1 * q2 * m4 + q2 * q2 * m5
    a2 = alpha_of(rz2, curve2)
    return a0 + a1 * u + a2 * q0, a2 * q1 - a1 * a0, a2 * q2


def weigh(places, coefs, arrays, store):
    for r, n in chunks_of(arrays[0][0].shape[0]):
        part = slice(r, r + n)
        scale = [jnp.concatenate([c] * (n // 8), axis=0) for c in coefs]
        for i, at in enumerate(places):
            store(at, part, sum(c * a[i][part] for c, a in zip(scale, arrays)))


def fetch_all(stored, fetched, arrived, width):
    copies = [pltpu.make_async_copy(x, fetched.at[k], arrived.at[k]) for k, x in enumerate(stored)]
    for copy in copies:
        copy.start()
    return copies, [[fetched.at[k * width + i] for i in range(width)] for k in range(3)]


def gradient_sum_kernel(width, place, told_ref, *refs):
    stored, (gradient_ref, coef_ref, fetched, arrived) = refs[: 3 * width], refs[3 * width :]
    copies, terms = fetch_all(stored, fetched, arrived, width)
    sums = least = told_ref[0]
    for k in range(1, told_ref.shape[0]):
        sums = sums + told_ref[k]
        least = jnp.minimum(least, told_ref[k])
    sums = jnp.sum(sums, axis=1, keepdims=True)
    least = jnp.min(least, axis=1, keepdims=True)
    coefs = combine([sums[i : i + 1] for i in range(6)], least[6:7])
    depth = coef_ref.shape[1]
    for k, c in enumerate(coefs):
        coef_ref[8 * k : 8 * k + 8] = jnp.broadcast_to(c, (8, depth))
    for copy in copies:
        copy.wait()

    def store(at, part, value):
        gradient_ref[at, part] = value

    weigh([plane_at(i, width, place[3]) for i in range(width)], [jnp.broadcast_to(-c, (8, depth)) for c in coefs], terms, store)


def lambda_kernel(width, place, coef_ref, *refs):
    stored, (adjoint_ref, fetched, arrived) = refs[: 3 * width], refs[3 * width :]
    copies, fields = fetch_all(stored, fetched, arrived, width)
    for copy in copies:
        copy.wait()

    def store(at, part, value):
        adjoint_ref[0, at, part] = value

    weigh([plane_at(i, width, place[3]) for i in range(width)], [coef_ref[8 * k : 8 * k + 8] for k in range(3)], fields, store)


def deliver_kernel(place, own_ref, beside_ref, other_ref, handed_ref, kept_ref, moved_ref, gradient_ref, adjoint_ref):
    for i in range(gradient_ref.shape[0]):
        for r, n in chunks_of(gradient_ref.shape[1]):
            part = slice(r, r + n)
            here = pick(place, own_ref[i, part], beside_ref[i, part])
            gradient_ref[i, part] = here + pick(place, handed_ref[i, part], other_ref[i, part])
            adjoint_ref[0, i, part] = pick(place, kept_ref[0, i, part], moved_ref[0, i, part])


BOTH = ("test", "slab")


def on_device(
    log_conductivity, storage, active_mask, heads, adjoint_next, pump_cells, obs_cells, obs_data
):
    width, rows, depth = log_conductivity.shape
    plane, stack = (rows, depth), (width, rows, depth)
    slabs = lax.axis_size("slab")
    cells_here = width * rows * depth
    turned = lax.axis_size("test") == 2 and slabs % 2 == 0
    if turned:
        pairs = [(slabs + 2 * j, 2 * j + 1) for j in range(slabs // 2)]
        far_pairs = [(slabs + i, i + 2) for i in range(slabs - 2)]
        near_axis, near = "test", [(0, 1), (1, 0)]
        far_axis = BOTH
        same_test = [[t * slabs + i for t in range(2) for i in range(x, slabs, 2)] for x in range(2)]
        at = lambda t, i: t * slabs + i
        first_far = [
            way
            for j in range(0, slabs - 2, 2)
            for way in (
                (at(0, j + 2), at(1, j)),
                (at(1, j + 2), at(1, j + 1)),
                (at(0, j + 1), at(0, j + 2)),
                (at(1, j + 1), at(0, j + 3)),
            )
        ]
    else:
        pairs = []
        far_pairs = [(i, i + 1) for i in range(1, slabs - 1, 2)]
        near_axis, near = "slab", [(i, i ^ 1) for i in range(slabs) if i ^ 1 < slabs]
        far_axis, same_test = "slab", None
    both_ways = lambda links: [way for a, b in links for way in ((a, b), (b, a))]
    if not turned:
        first_far = both_ways(far_pairs)

    def position():
        place, test = lax.axis_index("slab"), lax.axis_index("test")
        parity = lax.rem(place, 2)
        flip, mine = (test, place - parity + test) if turned else (parity, place)
        far_partner, near_partner = mine - 1 + 2 * flip, mine + 1 - 2 * flip
        return [
            place * cells_here,
            (far_partner >= 0) & (far_partner < slabs),
            near_partner < slabs,
            flip,
            mine != place,
            parity if turned else 0,
            test if turned else 0,
            parity,
        ]

    def move(x):
        return lax.ppermute(x, BOTH, both_ways(pairs)) if turned else x

    def swap_near(x):
        return lax.ppermute(x, near_axis, near)

    def swap_far(x):
        return lax.ppermute(x, far_axis, both_ways(far_pairs))

    def after(x, *others):
        return lax.optimization_barrier((x, others))[0]

    hbm = lambda *shape: pltpu.HBM(shape, jnp.float32)
    planes = [plane] * width

    far_at = plane_at(0, width, position()[7])
    far_plane = lambda x: lax.dynamic_slice(x, (far_at, 0, 0), (1, rows, depth))[0]
    log_moved = move(log_conductivity)
    def native(first, count):
        return call(
            lambda *refs: native_kernel(width, first, count, position(), *refs),
            [pump_cells, obs_cells, obs_data[0], storage, active_mask, heads, adjoint_next],
            [(2 * count, rows, depth)] + [(1, *stack)] * (first > 0),
            scalars=3,
            space=pltpu.HBM,
        )

    (far_pack,), (near_pack, heads_here) = native(0, 1), native(1, width - 1)
    far_moved = move(far_pack)
    log_halo = lax.ppermute(after(far_plane(log_conductivity), far_pack), far_axis, first_far)
    cond = call(
        lambda *refs: cond_kernel(width, position(), *refs),
        [log_conductivity, log_moved],
        planes,
        space=None,
    )
    cond_halo = [log_halo, swap_near(cond[-1])]
    near_moved = move(after(near_pack, *cond, log_halo))
    total, faces = (lambda x: (x[:width], x[width:]))(
        call(lambda *refs: face_kernel(width, *refs), cond, planes * (1 + SIDES) + [plane] * (width - 1))
    )
    def start(first, count, ends, pack, pack_moved):
        started = call(
            lambda *refs: start_kernel(count, ends, position(), *refs),
            [pack, pack_moved, *(cond_halo[side] for _, side in ends), *cond[first:][:count], *total[first:][:count]],
            [plane] * (3 * count + len(ends)) + [(8, depth)] * 2 + [(rows + SPARE, depth)] * (not first),
        )
        return [*(started[k * count : (k + 1) * count] for k in range(3)), started[3 * count :]]

    field, inverse, own, (outer_far, sum_far, least_far, send) = start(0, 1, [(0, 0)], far_pack, far_moved)
    v_halo = swap_far(send)
    field_near, inverse_near, own_near, (outer_near, sum_near, least_near) = start(
        1, width - 1, [(width - 2, 1)], near_pack, near_moved
    )
    field, inverse, own = [*field, *field_near], [*inverse, *inverse_near], [*own, *own_near]
    outer = [outer_far, outer_near]

    sums, fields, halos = [sum_far, sum_near], [], []
    for step in range(3):
        halo = [swap_far(field[0]) if step else v_halo, swap_near(field[-1])]
        fields += field
        image = call(lambda *refs: inner_kernel(width, *refs), [*field, *own, *faces], planes, cost=(1 << 23) if step == 1 else COST)
        if step == HEADS_STEP:
            heads_moved = move(after(heads_here, *image))
        if step == 1:
            heads_moved = after(heads_moved, *image)
            head = call(lambda *refs: head_kernel(width, position(), *refs), [heads_here, heads_moved], planes, space=None)
            head_far, head_near = swap_far(head[0]), swap_near(head[-1])
        if step < 2:
            halos += halo
            made = call(
                lambda *refs: finish_kernel(width, *refs),
                [*image, *field, *inverse, *outer, *halo],
                planes + [(8, depth)] * 2,
            )
            field, (odd, even) = made[:width], made[width:]
            sums += [odd, even]
    *terms, weight_0, weight_1 = call(
        lambda *refs: gradient_kernel(width, *refs),
        [*cond, *head, *faces, *outer, head_far, head_near, *fields, *halos],
        [hbm(*plane)] * (2 * width) + planes + [plane] * 2,
    )
    told, *last_terms = call(
        lambda *refs: last_kernel(width, *refs),
        [*image, *field, *terms[2 * width :], *outer, *halo, weight_0, weight_1, *sums, least_far, least_near],
        [hbm(slabs, 8, depth)] + [hbm(*plane)] * width,
        cost=1 << 24,
    )
    told = lax.all_to_all(told, far_axis, 0, 0, axis_index_groups=same_test, tiled=True)
    fetching = dict(
        space=None,
        stored=3 * width,
        scratch=[VMEM((3 * width, rows, depth), jnp.float32), pltpu.SemaphoreType.DMA((3 * width,))],
    )
    gradient, coefs = call(
        lambda *refs: gradient_sum_kernel(width, position(), *refs),
        [told, *(pltpu.with_memory_space_constraint(x, pltpu.HBM) for x in (*terms[: 2 * width], *last_terms))],
        [stack, (24, depth)],
        **fetching,
    )
    (adjoint,) = call(
        lambda *refs: lambda_kernel(width, position(), *refs),
        [coefs, *fields],
        [(1, *stack) if turned else jax.ShapeDtypeStruct((1, *stack), jnp.float32)],
        **fetching,
    )
    if turned:
        other = move(gradient)
        beside = lax.ppermute(gradient, "test", near)
        handed = lax.ppermute(other, "test", near)
        gradient, adjoint = call(
            lambda *refs: deliver_kernel(position(), *refs),
            [gradient, beside, other, handed, adjoint, move(adjoint)],
            [jax.ShapeDtypeStruct(shape, jnp.float32) for shape in (stack, (1, *stack))],
        )
    else:
        gradient = lax.psum(gradient, "test")
    return adjoint, gradient


def solution(mesh):
    return jax.shard_map(
        on_device,
        mesh=mesh,
        in_specs=(
            P("slab", None, None),
            P("slab", None, None),
            P("slab", None, None),
            P("test", "slab", None, None),
            P("test", "slab", None, None),
            P("test"),
            P(),
            P("test", None),
        ),
        out_specs=(P("test", "slab", None, None), P("slab", None, None)),
        check_vma=False,
    )
```
